32 devices in a mesh: dp: 8 (over y, x, core), mp: 4 (over z).
Axes of the slice: x: 2, y: 2, z: 4, core: 2. Of those that a mesh axis runs over, the one named last changes fastest.
Arguments:
- tokens: bfloat16 [4096, 2048], P(('dp', 'mp')), may hold values from -6 to 6
- lengths: int32 [8], P('dp'), may hold values from 128 to 512, as said below
- w_query: bfloat16 [2048, 256], P(None, 'mp'), may hold values from -0.125 to 0.125
- w_key: bfloat16 [2048, 256], P(None, 'mp'), may hold values from -0.125 to 0.125
- w_value: bfloat16 [2048, 2048], P(None, 'mp'), may hold values from -0.125 to 0.125
- w_out: bfloat16 [2048, 2048], P('mp'), may hold values from -3 to 3
- w_gate: bfloat16 [2048, 5504], P(None, 'mp'), may hold values from -0.125 to 0.125
- w_up: bfloat16 [2048, 5504], P(None, 'mp'), may hold values from -0.125 to 0.125
- w_down: bfloat16 [5504, 2048], P('mp'), may hold values from -0.078125 to 0.078125
- gain_attn: float32 [2048], replicated, may hold values from 0.5 to 1.5
- gain_mlp: float32 [2048], replicated, may hold values from 0.5 to 1.5
- out_cotangent: bfloat16 [4096, 2048], P(('dp', 'mp')), may hold values from -7 to 7
Outputs:
- outputs: bfloat16 [4096, 2048], P(('dp', 'mp'))
- grad_tokens: float32 [4096, 2048], P(('dp', 'mp'))
- grad_query: float32 [2048, 256], P('dp', 'mp')
- grad_key: float32 [2048, 256], P('dp', 'mp')
- grad_value: float32 [2048, 2048], P('dp', 'mp')
- grad_out_proj: float32 [2048, 2048], P('mp', 'dp')
- grad_gate: float32 [2048, 5504], P('dp', 'mp')
- grad_up: float32 [2048, 5504], P('dp', 'mp')
- grad_down: float32 [5504, 2048], P('mp', 'dp')
- grad_gain_attn: float32 [2048], replicated
- grad_gain_mlp: float32 [2048], replicated
The draws below stay inside these ranges and needn't reach their ends.
Inputs may be any that keep to these rules, and one draw needn't show every extreme that they name: Each row's live tokens are its first lengths[i]; in every draw some row is full.
All inputs are finite; a program needn't handle non-finite values.
Results may differ from the reference program's by a relative error of at most 0.017.
Values may be sent and summed in bfloat16 or wider, within the bound.
No kernel may reach another device: no remote copies, remote signals or barrier semaphores. Data moves between devices by JAX's collectives and lax.ppermute only.
A program may use at most 192 MiB of HBM per device.

```python
import jax
import jax.numpy as jnp
from jax import lax

D = 2048
H = 16
FK = 16
DV = 128
FF = 5504
ROW = 512
TOKENS = 4096
N_DP = 8


def draw_lengths(key, part):
    key = jax.random.fold_in(key, 11)
    drawn = jax.random.randint(key, (N_DP,), ROW // 4, ROW + 1, dtype=jnp.int32)
    chosen = jax.random.randint(jax.random.fold_in(key, 1), (), 0, N_DP, dtype=jnp.int32)
    return jnp.where(jnp.arange(N_DP, dtype=jnp.int32) == chosen, ROW, drawn).astype(jnp.int32)


def draw_out_cotangent(key, part):
    key = jax.random.fold_in(key, 23)
    ramp = jnp.arange(TOKENS, dtype=jnp.float32) / TOKENS
    scale = 0.5 + ramp
    base = jnp.clip(jax.random.normal(key, (TOKENS, D), jnp.float32), -4.0, 4.0)
    return (base * scale[:, None]).astype(jnp.bfloat16)


def block_levels(key, shape, cuts, low, top_value):
    def one(axis_at, parts):
        heights = jax.random.uniform(jax.random.fold_in(jax.random.fold_in(key, 6), axis_at), (parts,), jnp.float32, low / len(cuts), top_value / len(cuts))
        return jnp.repeat(jnp.exp(heights), shape[axis_at] // parts).reshape((-1,) + (1,) * (len(shape) - axis_at - 1))

    level = one(*cuts[0])
    for cut in cuts[1:]:
        level = level * one(*cut)
    return level


def bell_draw(own_key, shape, width, limit, cuts=(), kind=jnp.bfloat16):
    loudness = block_levels(own_key, shape, cuts, -0.22, 0.18) if cuts else 1.0
    values = jax.random.normal(own_key, shape, jnp.float32) * width * loudness
    return jnp.minimum(jnp.maximum(values, -limit), limit).astype(kind)


def setup_inputs(seed: int = 0) -> dict:
    streams_of = jax.random.split(jax.random.key(seed), 13)
    tokens = bell_draw(streams_of[0], (TOKENS, D), 1.0, 6.0, ((0, 32),))
    lengths = draw_lengths(jax.random.fold_in(streams_of[12], 71), 0)
    w_query = bell_draw(streams_of[2], (D, H * FK), D ** -0.5, 0.125, ((1, 4),))
    w_key = bell_draw(streams_of[3], (D, H * FK), D ** -0.5, 0.125, ((1, 4),))
    w_value = bell_draw(streams_of[4], (D, H * DV), D ** -0.5, 0.125, ((1, 4),))
    w_out = bell_draw(streams_of[5], (H * DV, D), (max(H * DV // ROW, 1)) ** -0.5, 3.0, ((0, 4),))
    w_gate = bell_draw(streams_of[6], (D, FF), D ** -0.5, 0.125, ((1, 4),))
    w_up = bell_draw(streams_of[7], (D, FF), D ** -0.5, 0.125, ((1, 4),))
    w_down = bell_draw(streams_of[8], (FF, D), FF ** -0.5, 0.078125, ((0, 4),))
    gain_attn = jnp.clip(1.0 + 0.1 * jax.random.normal(streams_of[9], (D,), jnp.float32), 0.5, 1.5)
    gain_mlp = jnp.clip(1.0 + 0.1 * jax.random.normal(streams_of[10], (D,), jnp.float32), 0.5, 1.5)
    out_cotangent = draw_out_cotangent(jax.random.fold_in(streams_of[12], 71), 0)
    return {"tokens": tokens, "lengths": lengths, "w_query": w_query, "w_key": w_key, "w_value": w_value, "w_out": w_out, "w_gate": w_gate, "w_up": w_up, "w_down": w_down, "gain_attn": gain_attn, "gain_mlp": gain_mlp, "out_cotangent": out_cotangent}


EPSILON = 1e-06

@jax.custom_vjp
def low(v):
    return lax.optimization_barrier(v.astype(jnp.bfloat16)).astype(jnp.float32)

@jax.custom_vjp
def lower_backward(v):
    return v

def low_keep(v):
    return (low(v), None)

def low_pass(kept, grad):
    return (grad,)

def back_keep(v):
    return (v, None)

def back_low(kept, grad):
    return (low(grad),)
low.defvjp(low_keep, low_pass)
lower_backward.defvjp(back_keep, back_low)

def matmul(left, right):
    return jnp.dot(left, right, precision=lax.Precision.HIGHEST)

def rms_scale(values):
    return lax.rsqrt(lax.optimization_barrier(jnp.mean(values * values, axis=-1, keepdims=True)) + EPSILON)

def row_layer(inputs, length, w_query, w_key, w_value, w_out, w_gate, w_up, w_down, gain_attn, gain_mlp):
    scale_one = rms_scale(inputs)
    normed = low(inputs * scale_one * gain_attn)
    query_rows = lower_backward(low(matmul(normed, w_query))).reshape(ROW, H, FK)
    key_rows = lower_backward(low(matmul(normed, w_key))).reshape(ROW, H, FK)
    values = lower_backward(low(matmul(normed, w_value))).reshape(ROW, H, DV)
    inner_product = lower_backward(jnp.einsum('dun,sun->uds', query_rows, key_rows, precision=lax.Precision.HIGHEST))
    places = jnp.arange(ROW, dtype=jnp.int32)
    visible = (places[None, :] <= places[:, None]) & (places[None, :] < length)
    weight = jnp.where(visible[None], 1.0 + inner_product * 0.25 + inner_product * inner_product * (1.0 / 32.0), 0.0)
    share = low(weight / lax.optimization_barrier(jnp.sum(weight, axis=-1, keepdims=True)))
    mixed = jnp.einsum('hqk,khe->qhe', share, values, precision=lax.Precision.HIGHEST).reshape(ROW, H * DV)
    mixed = lower_backward(low(mixed))
    resid = inputs + lower_backward(matmul(mixed, w_out))
    scale_two = rms_scale(resid)
    normed_two = low(resid * scale_two * gain_mlp)
    gate = lower_backward(matmul(normed_two, w_gate))
    upward = lower_backward(matmul(normed_two, w_up))
    hidden = lower_backward(low(jax.nn.silu(gate) * upward))
    return resid + lower_backward(matmul(hidden, w_down))

def reference(tokens, lengths, w_query, w_key, w_value, w_out, w_gate, w_up, w_down, gain_attn, gain_mlp, out_cotangent):

    def forward(inputs, wq_full, wk_full, wv_full, wo_full, wg_full, wu_full, wd_full, gain_one, gain_two):
        row_stack = inputs.reshape(N_DP, ROW, D)

        def one_row(item):
            row_inputs, length = item
            return row_layer(row_inputs, length, wq_full, wk_full, wv_full, wo_full, wg_full, wu_full, wd_full, gain_one, gain_two)
        return lax.map(jax.checkpoint(one_row), (row_stack, lengths)).reshape(N_DP * ROW, D)
    primal = (tokens.astype(jnp.float32), w_query.astype(jnp.float32), w_key.astype(jnp.float32), w_value.astype(jnp.float32), w_out.astype(jnp.float32), w_gate.astype(jnp.float32), w_up.astype(jnp.float32), w_down.astype(jnp.float32), gain_attn, gain_mlp)
    result, pullback = jax.vjp(forward, *primal)
    grads = pullback(out_cotangent.astype(jnp.float32))
    return (result.astype(jnp.bfloat16), grads[0], grads[1], grads[2], grads[3], grads[4], grads[5], grads[6], grads[7], grads[8], grads[9])
```

```python
import jax
import jax.numpy as jnp
from jax import lax
from jax.sharding import PartitionSpec as P

FK = 16
DV = 128
EPSILON = 1e-06

BF = jnp.bfloat16
F32 = jnp.float32

PAIRS = [(0, 1), (1, 0), (2, 3), (3, 2)]
MIDDLE = [(1, 2), (2, 1)]
OUTWARD = [(2, 3), (1, 0)]
INWARD = [(3, 2), (0, 1)]


def dot(left, right):
    return jnp.dot(left, right, preferred_element_type=F32)


def dot_nt(left, right):
    return lax.dot_general(left, right, (((1,), (1,)), ((), ())), preferred_element_type=F32)


def dot_tn(left, right):
    return lax.dot_general(left, right, (((0,), (0,)), ((), ())), preferred_element_type=F32)


def chain_gather(own, is_middle):
    one = lax.ppermute(own, "mp", PAIRS)
    near = lax.ppermute(own, "mp", MIDDLE)
    two = lax.ppermute(near, "mp", OUTWARD)
    far = lax.ppermute(one, "mp", MIDDLE)
    three = lax.ppermute(far, "mp", OUTWARD)
    return [own, one, jnp.where(is_middle, near, two), jnp.where(is_middle, far, three)]


def chain_scatter(part):
    third = part(3).astype(BF)
    from_edge = lax.ppermute(third, "mp", INWARD)
    second = part(2).astype(BF)
    from_edge_two = lax.ppermute(second, "mp", INWARD)
    across = lax.ppermute(third + from_edge, "mp", MIDDLE)
    first = part(1)
    pair = lax.ppermute((first + across.astype(F32)).astype(BF), "mp", PAIRS)
    near = lax.ppermute(second + from_edge_two, "mp", MIDDLE)
    return part(0) + pair.astype(F32) + near.astype(F32)


def on_device(
    tokens,
    lengths,
    w_query,
    w_key,
    w_value,
    w_out,
    w_gate,
    w_up,
    w_down,
    gain_attn,
    gain_mlp,
    out_cotangent,
):
    shard = tokens.shape[0]
    width = tokens.shape[1]
    full = shard * 4
    heads = w_query.shape[1] // FK
    n_dp = lax.axis_size("dp")
    block = width // n_dp
    bits = [1 << b for b in range(n_dp.bit_length() - 1)]
    me_mp = lax.axis_index("mp")
    me_dp = lax.axis_index("dp")
    is_middle = (me_mp == 1) | (me_mp == 2)
    length = lengths[0]
    chunk_ids = [
        me_mp,
        me_mp ^ 1,
        jnp.where(is_middle, me_mp ^ 3, me_mp ^ 2),
        jnp.where(is_middle, me_mp ^ 2, me_mp ^ 3),
    ]
    places = jnp.concatenate(
        [c * shard + jnp.arange(shard, dtype=jnp.int32) for c in chunk_ids]
    )
    visible = (places[None, :] <= places[:, None]) & (places[None, :] < length)

    def swap_dp(value, bit):
        return lax.ppermute(value, "dp", [(i, i ^ bit) for i in range(n_dp)])

    def own_blocks(array, odd):
        cut = [
            lax.dynamic_slice_in_dim(array, (me_dp ^ k) * block, block, axis=1)
            for k in range(odd, n_dp, 2)
        ]
        return cut

    def both_rows(array):
        return jnp.concatenate([array, swap_dp(array, 1)], axis=0)

    def both_rows_blocks(array):
        mine = jnp.concatenate(own_blocks(array, 0), axis=1)
        theirs = swap_dp(jnp.concatenate(own_blocks(array, 1), axis=1), 1)
        joined = jnp.concatenate([mine, theirs], axis=0)
        return {
            k: joined[:, j * block : (j + 1) * block] for j, k in enumerate(range(0, n_dp, 2))
        }

    def scatter_dp(blocks, product, order):
        slots = list(range(0, n_dp, 2))
        bit = order[0]
        away = [k for k in slots if k & bit]
        keep = [k for k in slots if not k & bit]
        got = swap_dp(product([blocks[k] for k in away]).astype(BF), bit)
        have = product([blocks[k] for k in keep]) + got.astype(F32)
        for bit in order[1:]:
            axis_len = len(keep)
            index_away = [j for j, k in enumerate(keep) if k & bit]
            index_keep = [j for j, k in enumerate(keep) if not k & bit]
            got = swap_dp(have[jnp.array(index_away)].astype(BF), bit) if axis_len > 2 else swap_dp(
                have[index_away[0] : index_away[0] + 1].astype(BF), bit
            )
            have = (
                have[jnp.array(index_keep)] if axis_len > 2 else have[index_keep[0] : index_keep[0] + 1]
            ) + got.astype(F32)
            keep = [k for k in keep if not k & bit]
        return have[0]

    def rows_product(other):
        def product(chosen):
            return dot_tn(jnp.concatenate(chosen, axis=1), other).reshape(
                len(chosen), block, other.shape[1]
            )

        return product

    def columns_product(other):
        def product(chosen):
            return jnp.stack([dot_tn(other, c) for c in chosen])

        return product

    order_one = bits[1:]
    order_two = order_one[::-1]

    inputs = tokens.astype(F32)
    scale_one = lax.rsqrt(jnp.mean(inputs * inputs, axis=-1, keepdims=True) + EPSILON)
    normed = (inputs * scale_one * gain_attn).astype(BF)
    normed_slots = chain_gather(normed, is_middle)
    w_qkv = jnp.concatenate([w_query, w_key, w_value], axis=1)
    qkv = jnp.concatenate([dot(s, w_qkv).astype(BF) for s in normed_slots], axis=0)
    n_q = w_query.shape[1]
    query = qkv[:, :n_q].reshape(full, heads, FK)
    key = qkv[:, n_q : 2 * n_q].reshape(full, heads, FK)
    value = qkv[:, 2 * n_q :].reshape(full, heads, DV)

    def weights_of():
        inner = jnp.einsum("dun,sun->uds", query, key, preferred_element_type=F32)
        weight = jnp.where(
            visible[None], 1.0 + inner * 0.25 + inner * inner * (1.0 / 32.0), 0.0
        )
        return inner, weight

    inner, weight = weights_of()
    denominator = jnp.sum(weight, axis=-1, keepdims=True)
    share_exact = weight / denominator
    share = share_exact.astype(BF)
    mixed = (
        jnp.einsum("hqk,khe->qhe", share, value, preferred_element_type=F32)
        .astype(BF)
        .reshape(full, heads * DV)
    )

    def rows_of(array, slot):
        return array[slot * shard : (slot + 1) * shard]

    resid = inputs + chain_scatter(lambda k: dot(rows_of(mixed, k), w_out))

    cot_all = lax.all_gather(out_cotangent, "mp", axis=0, tiled=True)
    cot_full = jnp.concatenate(
        [lax.dynamic_slice_in_dim(cot_all, c * shard, shard, axis=0) for c in chunk_ids]
    )
    d_hidden = dot_nt(cot_full, w_down).astype(BF)

    scale_two = lax.rsqrt(jnp.mean(resid * resid, axis=-1, keepdims=True) + EPSILON)
    normed_two = (resid * scale_two * gain_mlp).astype(BF)
    second_slots = chain_gather(normed_two, is_middle)
    hidden_s, d_gate_s, d_up_s = [], [], []
    for k in range(4):
        gate = dot(second_slots[k], w_gate)
        upward = dot(second_slots[k], w_up)
        sig = jax.nn.sigmoid(gate)
        active = gate * sig
        back = rows_of(d_hidden, k).astype(F32)
        hidden_s.append((active * upward).astype(BF))
        d_gate_s.append((back * upward * sig * (1.0 + gate * (1.0 - sig))).astype(BF))
        d_up_s.append((back * active).astype(BF))

    d_normed_two = chain_scatter(lambda k: dot_nt(d_gate_s[k], w_gate) + dot_nt(d_up_s[k], w_up))

    hidden = jnp.concatenate(hidden_s, axis=0)
    d_gate = jnp.concatenate(d_gate_s, axis=0)
    d_up = jnp.concatenate(d_up_s, axis=0)
    second_full = jnp.concatenate(second_slots, axis=0)
    outputs = (resid + chain_scatter(lambda k: dot(hidden_s[k], w_down))).astype(BF)

    hidden_both = both_rows(hidden)
    cot_blocks = both_rows_blocks(cot_full)
    second_blocks = both_rows_blocks(second_full)
    grad_down = scatter_dp(cot_blocks, columns_product(hidden_both), order_one)
    grad_gate = scatter_dp(second_blocks, rows_product(both_rows(d_gate)), order_two)
    grad_up = scatter_dp(second_blocks, rows_product(both_rows(d_up)), order_one)

    gain_two_part = jnp.sum(d_normed_two * resid * scale_two, axis=0)
    weighted_two = d_normed_two * gain_mlp
    d_resid = (
        out_cotangent.astype(F32)
        + scale_two * weighted_two
        - resid * scale_two**3 * jnp.mean(weighted_two * resid, axis=-1, keepdims=True)
    )
    d_attn = d_resid.astype(BF)
    attn_full = jnp.concatenate(chain_gather(d_attn, is_middle), axis=0)
    d_mixed = dot_nt(attn_full, w_out).astype(BF)
    grad_out = scatter_dp(
        both_rows_blocks(attn_full), columns_product(both_rows(mixed)), order_two
    )

    d_heads = d_mixed.reshape(full, heads, DV)
    d_share = jnp.einsum("qhe,khe->hqk", d_heads, value, preferred_element_type=F32)
    d_value = jnp.einsum("hqk,qhe->khe", share, d_heads, preferred_element_type=F32)
    d_weight = (d_share - jnp.sum(d_share * share_exact, axis=-1, keepdims=True)) / denominator
    d_inner = jnp.where(visible[None], d_weight * (0.25 + inner * (1.0 / 16.0)), 0.0).astype(BF)
    d_query = jnp.einsum("hqk,khn->qhn", d_inner, key, preferred_element_type=F32)
    d_key = jnp.einsum("hqk,qhn->khn", d_inner, query, preferred_element_type=F32)
    d_qkv = jnp.concatenate(
        [
            d_query.astype(BF).reshape(full, heads * FK),
            d_key.astype(BF).reshape(full, heads * FK),
            d_value.astype(BF).reshape(full, heads * DV),
        ],
        axis=1,
    )
    normed_full = jnp.concatenate(normed_slots, axis=0)
    d_normed = chain_scatter(lambda k: dot_nt(rows_of(d_qkv, k), w_qkv))
    grad_qkv = scatter_dp(
        both_rows_blocks(normed_full), rows_product(both_rows(d_qkv)), order_one
    )

    gain_one_part = jnp.sum(d_normed * inputs * scale_one, axis=0)
    weighted_one = d_normed * gain_attn
    grad_tokens = (
        d_resid
        + scale_one * weighted_one
        - inputs * scale_one**3 * jnp.mean(weighted_one * inputs, axis=-1, keepdims=True)
    )
    gains = jnp.stack([gain_one_part, gain_two_part])
    for bit in bits:
        gains = gains + swap_dp(gains, bit)
    for bit in (1, 2):
        gains = gains + lax.ppermute(gains, "mp", [(i, i ^ bit) for i in range(4)])
    return (
        outputs,
        grad_tokens,
        grad_qkv[:, :n_q],
        grad_qkv[:, n_q : 2 * n_q],
        grad_qkv[:, 2 * n_q :],
        grad_out,
        grad_gate,
        grad_up,
        grad_down,
        gains[0],
        gains[1],
    )


def solution(mesh):
    return jax.shard_map(
        on_device,
        mesh=mesh,
        in_specs=(
            P(("dp", "mp"), None),
            P("dp"),
            P(None, "mp"),
            P(None, "mp"),
            P(None, "mp"),
            P("mp", None),
            P(None, "mp"),
            P(None, "mp"),
            P("mp", None),
            P(),
            P(),
            P(("dp", "mp"), None),
        ),
        out_specs=(
            P(("dp", "mp"), None),
            P(("dp", "mp"), None),
            P("dp", "mp"),
            P("dp", "mp"),
            P("dp", "mp"),
            P("mp", "dp"),
            P("dp", "mp"),
            P("dp", "mp"),
            P("mp", "dp"),
            P(),
            P(),
        ),
        check_vma=False,
    )
```

```python
import functools

import jax
import jax.numpy as jnp
from jax import lax
from jax.experimental import pallas as pl
from jax.experimental.pallas import tpu as pltpu
from jax.sharding import PartitionSpec as P

FK = 16
DV = 128
BF = jnp.bfloat16
F32 = jnp.float32
EPSILON = 1e-06
BLOCK = 128
UNSEEN = 1 << 24

PAIRS = [(0, 1), (1, 0), (2, 3), (3, 2)]
MIDDLE = [(1, 2), (2, 1)]
OUTWARD = [(2, 3), (1, 0)]
INWARD = [(3, 2), (0, 1)]


def dot(left, right):
    return jnp.dot(left, right, preferred_element_type=F32)


def dot_nt(left, right):
    return lax.dot_general(left, right, (((1,), (1,)), ((), ())), preferred_element_type=F32)


def dot_tn(left, right):
    return lax.dot_general(left, right, (((0,), (0,)), ((), ())), preferred_element_type=F32)


def head_lanes(array, head):
    lane = lax.broadcasted_iota(jnp.int32, array.shape, 1) // FK
    return jnp.where(lane == head, array.astype(F32), 0.0).astype(BF)


def weights_of(query, key, seen):
    inner = dot_nt(query, key)
    weight = jnp.where(seen, 1.0 + inner * (0.25 + inner * (1.0 / 32.0)), 0.0)
    return inner, weight, 1.0 / jnp.sum(weight, axis=-1, keepdims=True)


def attention_kernel(heads, place_ref, bound_ref, qkv_ref, mixed_ref):
    n_q = heads * FK
    key = qkv_ref[:, n_q : 2 * n_q]
    queries = [head_lanes(qkv_ref[:, :n_q], h) for h in range(heads)]
    bound = bound_ref[...]
    for first in range(0, qkv_ref.shape[0], BLOCK):
        seen = bound <= place_ref[first : first + BLOCK]
        for h in range(heads):
            _, weight, scale = weights_of(queries[h][first : first + BLOCK], key, seen)
            value = qkv_ref[:, 2 * n_q + h * DV : 2 * n_q + (h + 1) * DV]
            mixed_ref[first : first + BLOCK, h * DV : (h + 1) * DV] = dot(
                (weight * scale).astype(BF), value
            ).astype(BF)


def attention(place, bound, qkv):
    heads = (qkv.shape[1] // (2 * FK + DV))
    return pl.pallas_call(
        functools.partial(attention_kernel, heads),
        out_shape=jax.ShapeDtypeStruct((qkv.shape[0], heads * DV), BF),
        compiler_params=pltpu.CompilerParams(vmem_limit_bytes=32 * 2**20),
        name="attention",
    )(place, bound, qkv)


def attention_back_kernel(heads, start, last, *refs):
    if last:
        place_ref, bound_ref, qkv_ref, d_mixed_ref, query_ref, total_ref, out_ref = refs
    else:
        place_ref, bound_ref, qkv_ref, d_mixed_ref, query_ref, total_ref = refs
    n_q = heads * FK
    key = qkv_ref[:, n_q : 2 * n_q]
    keys = [head_lanes(key, h) for h in range(heads)]
    bound = bound_ref[...]
    rows = d_mixed_ref.shape[0]
    d_key = 0.0
    d_values = [0.0] * heads
    for first in range(0, rows, BLOCK):
        here = slice(start + first, start + first + BLOCK)
        seen = bound <= place_ref[here]
        d_query = 0.0
        for h in range(heads):
            query = head_lanes(qkv_ref[here, :n_q], h)
            inner, weight, scale = weights_of(query, key, seen)
            share = weight * scale
            value = qkv_ref[:, 2 * n_q + h * DV : 2 * n_q + (h + 1) * DV]
            d_out = d_mixed_ref[first : first + BLOCK, h * DV : (h + 1) * DV]
            d_share = dot_nt(d_out, value)
            row = jnp.sum(d_share * share, axis=-1, keepdims=True)
            d_inner = jnp.where(
                seen, (d_share - row) * scale * (0.25 + inner * (1.0 / 16.0)), 0.0
            ).astype(BF)
            d_query = d_query + dot(d_inner, keys[h])
            d_key = d_key + dot_tn(d_inner, query)
            d_values[h] = d_values[h] + dot_tn(share.astype(BF), d_out)
        if last:
            out_ref[here, :n_q] = d_query.astype(BF)
        else:
            query_ref[first : first + BLOCK] = d_query.astype(BF)
    if last:
        out_ref[:start, :n_q] = query_ref[...]
        out_ref[:, n_q : 2 * n_q] = (d_key + total_ref[:, heads * DV :]).astype(BF)
        for h in range(heads):
            out_ref[:, 2 * n_q + h * DV : 2 * n_q + (h + 1) * DV] = (
                d_values[h] + total_ref[:, h * DV : (h + 1) * DV]
            ).astype(BF)
    else:
        total_ref[:, heads * DV :] = d_key
        for h in range(heads):
            total_ref[:, h * DV : (h + 1) * DV] = d_values[h]


def attention_back(place, bound, qkv, d_mixed, start, before):
    heads = (qkv.shape[1] // (2 * FK + DV))
    n_q = heads * FK
    rows = d_mixed.shape[0]
    last = before is not None
    if last:
        shape = jax.ShapeDtypeStruct(qkv.shape, BF)
    else:
        shape = (
            jax.ShapeDtypeStruct((rows, n_q), BF),
            jax.ShapeDtypeStruct((qkv.shape[0], n_q + heads * DV), F32),
        )
    return pl.pallas_call(
        functools.partial(attention_back_kernel, heads, start, last),
        out_shape=shape,
        compiler_params=pltpu.CompilerParams(vmem_limit_bytes=40 * 2**20),
        name="attention_back",
    )(place, bound, qkv, d_mixed, *(before or ()))


def after(value, *others):
    return lax.optimization_barrier((value, *others))[0]


def along(value, pairs):
    return lax.ppermute(value, "mp", pairs)


def on_device(
    tokens,
    lengths,
    w_query,
    w_key,
    w_value,
    w_out,
    w_gate,
    w_up,
    w_down,
    gain_attn,
    gain_mlp,
    out_cotangent,
):
    shard = tokens.shape[0]
    width = tokens.shape[1]
    heads = w_query.shape[1] // FK
    n_q = w_query.shape[1]
    n_dp = lax.axis_size("dp")
    block = width // n_dp
    bits = [1 << b for b in range(n_dp.bit_length() - 1)]
    me_mp = lax.axis_index("mp")
    me_dp = lax.axis_index("dp")
    is_middle = (me_mp == 1) | (me_mp == 2)
    chunk_ids = [
        me_mp,
        me_mp ^ 1,
        jnp.where(is_middle, me_mp ^ 3, me_mp ^ 2),
        jnp.where(is_middle, me_mp ^ 2, me_mp ^ 3),
    ]
    places = jnp.concatenate([c * shard + jnp.arange(shard, dtype=jnp.int32) for c in chunk_ids])
    bound = jnp.where(places < lengths[0], places, UNSEEN)[None, :]
    places = places[:, None]

    def rows_of(array, slot):
        return array[slot * shard : (slot + 1) * shard]

    def swap_dp(value, bit):
        return lax.ppermute(value, "dp", [(i, i ^ bit) for i in range(n_dp)])

    def both_rows(array):
        return jnp.concatenate([array, swap_dp(array, 1)], axis=0)

    def column_blocks(array, order):
        def pick(slots):
            return jnp.concatenate(
                [
                    lax.dynamic_slice_in_dim(array, (me_dp ^ k) * block, block, axis=1)
                    for k in slots
                ],
                axis=1,
            )

        even = range(0, n_dp, 2)
        away = [k for k in even if k & order[0]]
        stay = [k for k in even if not k & order[0]]
        for bit in order[:0:-1]:
            stay.sort(key=lambda k: bool(k & bit))
        for bit in order[:0:-1]:
            away.sort(key=lambda k: bool(k & bit))
        mine = pick(away + stay)
        theirs = swap_dp(pick([k ^ 1 for k in away + stay]), 1)
        joined = jnp.concatenate([mine, theirs], axis=0)
        half = len(away) * block
        return joined[:, :half], joined[:, half:]

    def halve(have, order, axis):
        for bit in order[1:]:
            half = have.shape[axis] // 2
            stay = lax.slice_in_dim(have, 0, half, axis=axis)
            away = lax.slice_in_dim(have, half, 2 * half, axis=axis)
            have = stay + swap_dp(away.astype(BF), bit).astype(F32)
        return have

    order_one = bits[1:]
    order_two = order_one[::-1]

    inputs = tokens.astype(F32)
    scale_one = lax.rsqrt(jnp.mean(inputs * inputs, axis=-1, keepdims=True) + EPSILON)
    normed = (inputs * scale_one * gain_attn).astype(BF)
    one = along(normed, PAIRS)
    near = along(normed, MIDDLE)
    w_qkv = jnp.concatenate([w_query, w_key, w_value], axis=1)
    qkv_0 = dot(normed, w_qkv).astype(BF)
    near, one = after(near, qkv_0), after(one, qkv_0)
    two = along(near, OUTWARD)
    far = along(one, MIDDLE)
    qkv_1 = dot(one, w_qkv).astype(BF)
    far, two = after(far, qkv_1), after(two, qkv_1)
    three = along(far, OUTWARD)
    cot_near = along(after(out_cotangent, far), MIDDLE)
    slot_2 = jnp.where(is_middle, near, two)
    qkv_2 = dot(slot_2, w_qkv).astype(BF)
    three = after(three, qkv_2)
    slot_3 = jnp.where(is_middle, far, three)
    cot_one = along(after(out_cotangent, three), PAIRS)
    qkv_3 = dot(slot_3, w_qkv).astype(BF)
    normed_slots = [normed, one, slot_2, slot_3]
    qkv = jnp.concatenate([qkv_0, qkv_1, qkv_2, qkv_3], axis=0)
    mixed = attention(places, bound, qkv)

    third = dot(rows_of(mixed, 3), w_out).astype(BF)
    edge = along(third, INWARD)
    cot_near, cot_one = after(cot_near, third), after(cot_one, third)
    cot_two = along(cot_near, OUTWARD)
    cot_far = along(cot_one, MIDDLE)
    second = dot(after(rows_of(mixed, 2), third), w_out).astype(BF)
    first = dot(after(rows_of(mixed, 1), third), w_out)
    zeroth = dot(after(rows_of(mixed, 0), third), w_out)
    edge = after(edge, second, first, zeroth)
    across = along(third + edge, MIDDLE)
    edge_two = along(after(second, edge), INWARD)
    cot_three = along(after(cot_far, edge), OUTWARD)
    mixed_both = both_rows(after(mixed, edge))
    normed_full = jnp.concatenate(normed_slots, axis=0)
    normed_away, normed_stay = column_blocks(after(normed_full, edge), order_one)
    across, edge_two = (
        after(across, mixed_both, normed_away, normed_stay),
        after(edge_two, mixed_both, normed_away, normed_stay),
    )
    pair = along((first + across.astype(F32)).astype(BF), PAIRS)
    middle = along(second + edge_two, MIDDLE)
    cot_full = jnp.concatenate(
        [
            out_cotangent,
            cot_one,
            jnp.where(is_middle, cot_near, cot_two),
            jnp.where(is_middle, cot_far, cot_three),
        ],
        axis=0,
    )
    d_hidden = dot_nt(after(cot_full, across), w_down).astype(BF)
    pair, middle = after(pair, d_hidden), after(middle, d_hidden)
    resid = inputs + (zeroth + pair.astype(F32) + middle.astype(F32))

    scale_two = lax.rsqrt(jnp.mean(resid * resid, axis=-1, keepdims=True) + EPSILON)
    normed_two = (resid * scale_two * gain_mlp).astype(BF)

    def feed(slot_rows, back):
        gate = dot(slot_rows, w_gate)
        upward = dot(slot_rows, w_up)
        sig = jax.nn.sigmoid(gate)
        active = gate * sig
        back = back.astype(F32)
        hid = (active * upward).astype(BF)
        d_g = (back * upward * sig * (1.0 + gate * (1.0 - sig))).astype(BF)
        d_u = (back * active).astype(BF)
        return hid, d_g, d_u

    def unfeed(fed):
        return dot_nt(fed[1], w_gate) + dot_nt(fed[2], w_up)

    one = along(normed_two, PAIRS)
    near = along(normed_two, MIDDLE)
    fed_0 = feed(normed_two, rows_of(d_hidden, 0))
    part_0 = unfeed(fed_0)
    cot_away, cot_stay = column_blocks(after(cot_full, normed_two), order_one)
    near, one = after(near, part_0, cot_away, cot_stay), after(one, part_0, cot_away, cot_stay)
    two = along(near, OUTWARD)
    far = along(one, MIDDLE)
    fed_1 = feed(one, rows_of(d_hidden, 1))
    part_1 = unfeed(fed_1)
    far, two = after(far, part_1), after(two, part_1)
    three = along(far, OUTWARD)
    slot_2 = jnp.where(is_middle, near, two)
    fed_2 = feed(slot_2, rows_of(d_hidden, 2))
    part_2 = unfeed(fed_2).astype(BF)
    three = after(three, part_2)
    slot_3 = jnp.where(is_middle, far, three)
    fed_3 = feed(slot_3, rows_of(d_hidden, 3))
    third = unfeed(fed_3).astype(BF)

    edge = along(third, INWARD)
    hidden_s, d_gate_s, d_up_s = zip(fed_0, fed_1, fed_2, fed_3)
    hidden_both = both_rows(after(jnp.concatenate(hidden_s, axis=0), third))
    second_full = jnp.concatenate([normed_two, one, slot_2, slot_3], axis=0)
    second_away, second_stay = column_blocks(after(second_full, third), order_two)
    up_away, up_stay = second_away, second_stay
    gate_both = both_rows(after(jnp.concatenate(d_gate_s, axis=0), third))
    up_both = both_rows(after(jnp.concatenate(d_up_s, axis=0), third))
    down_go = dot_tn(hidden_both, cot_away).astype(BF)
    down_got = swap_dp(down_go, order_one[0])
    edge = after(edge, down_go)
    across = along(third + edge, MIDDLE)
    edge_two = along(after(part_2, edge), INWARD)
    gate_go = dot_tn(after(second_away, edge), gate_both).astype(BF)
    gate_got = swap_dp(gate_go, order_two[0])
    up_go = dot_tn(after(up_away, edge), up_both).astype(BF)
    across, edge_two = after(across, gate_go, up_go), after(edge_two, gate_go, up_go)
    pair = along((part_1 + across.astype(F32)).astype(BF), PAIRS)
    middle = along(part_2 + edge_two, MIDDLE)
    up_got = swap_dp(after(up_go, across), order_two[0])
    out_3 = dot(after(fed_3[0], across), w_down).astype(BF)
    down_keep = dot_tn(hidden_both, after(cot_stay, across))
    pair = after(pair, out_3, down_keep)
    d_normed_two = part_0 + pair.astype(F32) + middle.astype(F32)
    weighted_two = d_normed_two * gain_mlp
    d_resid = (
        out_cotangent.astype(F32)
        + scale_two * weighted_two
        - resid * scale_two**3 * jnp.mean(weighted_two * resid, axis=-1, keepdims=True)
    )
    d_attn = d_resid.astype(BF)

    one = along(d_attn, PAIRS)
    near = along(d_attn, MIDDLE)
    gain_two_part = jnp.sum(d_normed_two * resid * scale_two, axis=0)
    out_2 = dot(after(fed_2[0], d_attn), w_down).astype(BF)
    out_1 = dot(after(fed_1[0], d_attn), w_down)
    out_0 = dot(after(fed_0[0], d_attn), w_down)
    gate_keep = dot_tn(after(second_stay, d_attn), gate_both)
    near, one = after(near, out_0, out_1, out_2, gate_keep), after(one, out_0, out_1, out_2, gate_keep)
    two = along(near, OUTWARD)
    far = along(one, MIDDLE)
    out_edge = along(after(out_3, one), INWARD)
    d_mixed_0 = dot_nt(after(d_attn, one), w_out).astype(BF)
    d_mixed_1 = dot_nt(one, w_out).astype(BF)
    up_keep = dot_tn(after(up_stay, one), up_both)
    down_mid = down_keep + after(down_got, one).astype(F32)
    grad_down = halve(down_mid, order_one, 1)
    far, two = after(far, d_mixed_1, up_keep), after(two, d_mixed_1, up_keep)
    three = along(far, OUTWARD)
    out_across = along(out_3 + out_edge, MIDDLE)
    out_edge_two = along(after(out_2, out_edge), INWARD)
    slot_2 = jnp.where(is_middle, near, two)
    d_mixed_2 = dot_nt(slot_2, w_out).astype(BF)
    before = attention_back(
        places, bound, qkv, jnp.concatenate([d_mixed_0, d_mixed_1, d_mixed_2], axis=0), 0, None
    )
    gate_mid = gate_keep + after(gate_got, far).astype(F32)
    grad_gate = halve(gate_mid, order_two, 0)
    three = after(three, before[0], gate_mid)
    slot_3 = jnp.where(is_middle, far, three)
    d_mixed_3 = dot_nt(slot_3, w_out).astype(BF)
    d_qkv = attention_back(places, bound, qkv, d_mixed_3, 3 * shard, before)

    third = dot_nt(rows_of(d_qkv, 3), w_qkv).astype(BF)
    edge = along(third, INWARD)
    out_pair = along(after((out_1 + out_across.astype(F32)).astype(BF), third), PAIRS)
    out_middle = along(after(out_2 + out_edge_two, third), MIDDLE)
    qkv_both = both_rows(after(d_qkv, third))
    attn_full = jnp.concatenate([d_attn, one, slot_2, slot_3], axis=0)
    attn_away, attn_stay = column_blocks(after(attn_full, third), order_two)
    second = dot_nt(after(rows_of(d_qkv, 2), third), w_qkv).astype(BF)
    first = dot_nt(after(rows_of(d_qkv, 1), third), w_qkv)
    zeroth = dot_nt(after(rows_of(d_qkv, 0), third), w_qkv)
    qkv_go = dot_tn(normed_away, qkv_both).astype(BF)
    qkv_got = swap_dp(qkv_go, order_one[0])
    out_go = dot_tn(mixed_both, attn_away).astype(BF)
    out_got = swap_dp(out_go, order_two[0])
    d_normed_part = jnp.concatenate([zeroth, first, second.astype(F32), third.astype(F32)], axis=0)
    gain_one_part = jnp.sum(d_normed_part * normed_full.astype(F32), axis=0) / gain_attn
    gains = jnp.stack([gain_one_part, gain_two_part])
    edge = after(edge, zeroth, first, second, qkv_go, out_go, gains)
    across = along(third + edge, MIDDLE)
    edge_two = along(after(second, edge), INWARD)
    gains = gains + swap_dp(after(gains, edge), bits[0])
    for bit in bits[1:]:
        gains = gains + swap_dp(gains, bit)
    up_mid = up_keep + after(up_got, edge).astype(F32)
    grad_up = halve(up_mid, order_two, 0)
    qkv_keep = dot_tn(after(normed_stay, edge), qkv_both)
    out_keep = dot_tn(mixed_both, after(attn_stay, edge))
    across, edge_two = (
        after(across, gains, up_mid, qkv_keep, out_keep),
        after(edge_two, gains, up_mid, qkv_keep, out_keep),
    )
    pair = along((first + across.astype(F32)).astype(BF), PAIRS)
    middle = along(second + edge_two, MIDDLE)
    for bit in (1, 2):
        gains = gains + along(after(gains, across), [(i, i ^ bit) for i in range(4)])
    grad_out = halve(out_keep + after(out_got, across).astype(F32), order_two, 1)
    grad_qkv = halve(qkv_keep + after(qkv_got, across).astype(F32), order_one, 0)
    outputs = (
        resid + (out_0 + after(out_pair, across).astype(F32) + out_middle.astype(F32))
    ).astype(BF)
    d_normed = zeroth + pair.astype(F32) + middle.astype(F32)
    weighted_one = d_normed * gain_attn
    grad_tokens = (
        d_resid
        + scale_one * weighted_one
        - inputs * scale_one**3 * jnp.mean(weighted_one * inputs, axis=-1, keepdims=True)
    )
    return (
        outputs,
        grad_tokens,
        grad_qkv[:, :n_q],
        grad_qkv[:, n_q : 2 * n_q],
        grad_qkv[:, 2 * n_q :],
        grad_out,
        grad_gate,
        grad_up,
        grad_down,
        gains[0],
        gains[1],
    )


def solution(mesh):
    return jax.shard_map(
        on_device,
        mesh=mesh,
        in_specs=(
            P(("dp", "mp"), None),
            P("dp"),
            P(None, "mp"),
            P(None, "mp"),
            P(None, "mp"),
            P("mp", None),
            P(None, "mp"),
            P(None, "mp"),
            P("mp", None),
            P(),
            P(),
            P(("dp", "mp"), None),
        ),
        out_specs=(
            P(("dp", "mp"), None),
            P(("dp", "mp"), None),
            P("dp", "mp"),
            P("dp", "mp"),
            P("dp", "mp"),
            P("mp", "dp"),
            P("dp", "mp"),
            P("dp", "mp"),
            P("mp", "dp"),
            P(),
            P(),
        ),
        check_vma=False,
    )
```

```python
import functools

import jax
import jax.numpy as jnp
from jax import lax
from jax.experimental import pallas as pl
from jax.experimental.pallas import tpu as pltpu
from jax.sharding import PartitionSpec as P

FK = 16
DV = 128
BF = jnp.bfloat16
F32 = jnp.float32
EPSILON = 1e-06
BLOCK = 128
UNSEEN = 1 << 24

PAIRS = [(0, 1), (1, 0), (2, 3), (3, 2)]
MIDDLE = [(1, 2), (2, 1)]
OUTWARD = [(2, 3), (1, 0)]
INWARD = [(3, 2), (0, 1)]


def dot(left, right):
    return jnp.dot(left, right, preferred_element_type=F32)


def dot_nt(left, right):
    return lax.dot_general(left, right, (((1,), (1,)), ((), ())), preferred_element_type=F32)


def dot_tn(left, right):
    return lax.dot_general(left, right, (((0,), (0,)), ((), ())), preferred_element_type=F32)


def head_lanes(array, head):
    lane = lax.broadcasted_iota(jnp.int32, array.shape, 1) // FK
    return jnp.where(lane == head, array.astype(F32), 0.0).astype(BF)


def weights_of(query, key, seen):
    inner = dot_nt(query, key)
    weight = jnp.where(seen, 1.0 + inner * (0.25 + inner * (1.0 / 32.0)), 0.0)
    return inner, weight, 1.0 / jnp.sum(weight, axis=-1, keepdims=True)


def attention_kernel(heads, place_ref, bound_ref, qkv_ref, mixed_ref):
    n_q = heads * FK
    key = qkv_ref[:, n_q : 2 * n_q]
    queries = [head_lanes(qkv_ref[:, :n_q], h) for h in range(heads)]
    bound = bound_ref[...]
    for first in range(0, qkv_ref.shape[0], BLOCK):
        seen = bound <= place_ref[first : first + BLOCK]
        for h in range(heads):
            _, weight, scale = weights_of(queries[h][first : first + BLOCK], key, seen)
            value = qkv_ref[:, 2 * n_q + h * DV : 2 * n_q + (h + 1) * DV]
            mixed_ref[first : first + BLOCK, h * DV : (h + 1) * DV] = dot(
                (weight * scale).astype(BF), value
            ).astype(BF)


def cost(flops):
    return pl.CostEstimate(flops=flops, bytes_accessed=2**21, transcendentals=0)


def attention(place, bound, qkv):
    heads = (qkv.shape[1] // (2 * FK + DV))
    return pl.pallas_call(
        functools.partial(attention_kernel, heads),
        out_shape=jax.ShapeDtypeStruct((qkv.shape[0], heads * DV), BF),
        compiler_params=pltpu.CompilerParams(vmem_limit_bytes=32 * 2**20),
        cost_estimate=cost(qkv.shape[0] * qkv.shape[0] * heads * 2 * (2 * FK + DV) * 16),
        name="attention",
    )(place, bound, qkv)


def attention_back_kernel(heads, start, last, *refs):
    if last:
        place_ref, bound_ref, qkv_ref, d_mixed_ref, query_ref, total_ref, out_ref = refs
    else:
        place_ref, bound_ref, qkv_ref, d_mixed_ref, query_ref, total_ref = refs
    n_q = heads * FK
    key = qkv_ref[:, n_q : 2 * n_q]
    keys = [head_lanes(key, h) for h in range(heads)]
    bound = bound_ref[...]
    rows = d_mixed_ref.shape[0]
    d_key = 0.0
    d_values = [0.0] * heads
    for first in range(0, rows, BLOCK):
        here = slice(start + first, start + first + BLOCK)
        seen = bound <= place_ref[here]
        d_query = 0.0
        for h in range(heads):
            query = head_lanes(qkv_ref[here, :n_q], h)
            inner, weight, scale = weights_of(query, key, seen)
            share = weight * scale
            value = qkv_ref[:, 2 * n_q + h * DV : 2 * n_q + (h + 1) * DV]
            d_out = d_mixed_ref[first : first + BLOCK, h * DV : (h + 1) * DV]
            d_share = dot_nt(d_out, value)
            row = jnp.sum(d_share * share, axis=-1, keepdims=True)
            d_inner = jnp.where(
                seen, (d_share - row) * scale * (0.25 + inner * (1.0 / 16.0)), 0.0
            ).astype(BF)
            d_query = d_query + dot(d_inner, keys[h])
            d_key = d_key + dot_tn(d_inner, query)
            d_values[h] = d_values[h] + dot_tn(share.astype(BF), d_out)
        if last:
            out_ref[here, :n_q] = d_query.astype(BF)
        else:
            query_ref[first : first + BLOCK] = d_query.astype(BF)
    if last:
        out_ref[:start, :n_q] = query_ref[...]
        out_ref[:, n_q : 2 * n_q] = (d_key + total_ref[:, heads * DV :]).astype(BF)
        for h in range(heads):
            out_ref[:, 2 * n_q + h * DV : 2 * n_q + (h + 1) * DV] = (
                d_values[h] + total_ref[:, h * DV : (h + 1) * DV]
            ).astype(BF)
    else:
        total_ref[:, heads * DV :] = d_key
        for h in range(heads):
            total_ref[:, h * DV : (h + 1) * DV] = d_values[h]


def attention_back(place, bound, qkv, d_mixed, start, before):
    heads = (qkv.shape[1] // (2 * FK + DV))
    n_q = heads * FK
    rows = d_mixed.shape[0]
    last = before is not None
    if last:
        shape = jax.ShapeDtypeStruct(qkv.shape, BF)
    else:
        shape = (
            jax.ShapeDtypeStruct((rows, n_q), BF),
            jax.ShapeDtypeStruct((qkv.shape[0], n_q + heads * DV), F32),
        )
    return pl.pallas_call(
        functools.partial(attention_back_kernel, heads, start, last),
        out_shape=shape,
        compiler_params=pltpu.CompilerParams(vmem_limit_bytes=40 * 2**20),
        cost_estimate=cost(rows * qkv.shape[0] * heads * 2 * (6 * FK + 2 * DV) * 16),
        name="attention_back",
    )(place, bound, qkv, d_mixed, *(before or ()))


def after(value, *others):
    return lax.optimization_barrier((value, *others))[0]


def along(value, pairs):
    return lax.ppermute(value, "mp", pairs)


def on_device(
    tokens,
    lengths,
    w_query,
    w_key,
    w_value,
    w_out,
    w_gate,
    w_up,
    w_down,
    gain_attn,
    gain_mlp,
    out_cotangent,
):
    shard = tokens.shape[0]
    width = tokens.shape[1]
    heads = w_query.shape[1] // FK
    n_q = w_query.shape[1]
    n_dp = lax.axis_size("dp")
    block = width // n_dp
    bits = [1 << b for b in range(n_dp.bit_length() - 1)]
    me_mp = lax.axis_index("mp")
    me_dp = lax.axis_index("dp")
    is_middle = (me_mp == 1) | (me_mp == 2)
    chunk_ids = [
        me_mp,
        me_mp ^ 1,
        jnp.where(is_middle, me_mp ^ 3, me_mp ^ 2),
        jnp.where(is_middle, me_mp ^ 2, me_mp ^ 3),
    ]
    places = jnp.concatenate([c * shard + jnp.arange(shard, dtype=jnp.int32) for c in chunk_ids])
    bound = jnp.where(places < lengths[0], places, UNSEEN)[None, :]
    places = places[:, None]

    order_one = bits[1:]
    order_two = order_one[::-1]
    even_slots = [2, 6, 4, 0] if n_dp == 8 else list(range(0, n_dp, 2))
    second_slots = [0, 2, 6, 4] if n_dp == 8 else list(range(0, n_dp, 2))

    def rows_of(array, slot):
        return array[slot * shard : (slot + 1) * shard]

    def exchange(outward, inward):
        return along(jnp.where(is_middle, outward, inward), PAIRS)

    def swap_dp(value, bit):
        return lax.ppermute(value, "dp", [(i, i ^ bit) for i in range(n_dp)])

    def both_rows(array):
        return jnp.concatenate([array, swap_dp(array, 1)], axis=0)

    def take(array, held, slots, axis, size=None):
        size = size or block
        at = [held.index(k) for k in slots]
        if at == list(range(at[0], at[0] + len(at))):
            return lax.slice_in_dim(array, at[0] * size, (at[-1] + 1) * size, axis=axis)
        return jnp.concatenate(
            [lax.slice_in_dim(array, i * size, (i + 1) * size, axis=axis) for i in at], axis=axis
        )

    def column_blocks(array):
        def pick(slots):
            return jnp.concatenate(
                [
                    lax.dynamic_slice_in_dim(array, (me_dp ^ k) * block, block, axis=1)
                    for k in slots
                ],
                axis=1,
            )

        theirs = swap_dp(pick([k ^ 1 for k in even_slots]), 1)
        return jnp.concatenate([pick(even_slots), theirs], axis=0)

    half = block // 2

    def half_columns(array):
        def pick(odd):
            cuts = [(k, 0) for k in even_slots] + [(k, half) for k in second_slots]
            return jnp.concatenate(
                [
                    lax.dynamic_slice_in_dim(
                        array, (me_dp ^ k ^ odd) * block + shift, half, axis=1
                    )
                    for k, shift in cuts
                ],
                axis=1,
            )

        joined = jnp.concatenate([pick(0), swap_dp(pick(1), 1)], axis=0)
        return joined

    def half_sums(columns, other, side, stage, gots):
        order = (order_one, order_two)[side]
        held = (even_slots, second_slots)[side]
        base = side * len(even_slots) * half
        cut = lax.slice_in_dim(columns, base, base + len(even_slots) * half, axis=1)
        slots = away_slots(order, stage)
        total = dot_tn(take(cut, held, slots, 1, half), other)
        for earlier, got in enumerate(gots):
            there = [k ^ order[earlier] for k in away_slots(order, earlier)]
            total = total + take(got, there, slots, 0, half).astype(F32)
        return total

    def send_halves(pair_of_halves, stage):
        return [
            swap_dp(part, order[stage])
            for part, order in zip(pair_of_halves, (order_one, order_two))
        ]

    def final_rows(columns, other, gots):
        last = len(order_one)
        parts = [half_sums(columns, other, side, last, gots[side]) for side in (0, 1)]
        return jnp.concatenate(parts, axis=0)

    def away_slots(order, stage):
        if stage == len(order):
            return [0]
        return [
            k for k in even_slots if k & order[stage] and not any(k & b for b in order[:stage])
        ]

    def block_sums(blocks, other, axis, order, gots):
        slots = away_slots(order, len(gots))
        picked = take(blocks, even_slots, slots, 1)
        total = dot_tn(picked, other) if axis == 0 else dot_tn(other, picked)
        for stage, got in enumerate(gots):
            held = [k ^ order[stage] for k in away_slots(order, stage)]
            total = total + take(got, held, slots, axis).astype(F32)
        return total

    def pass_on(sums, gots):
        blocks, other, axis, order = sums
        while True:
            go = block_sums(*sums, gots).astype(BF)
            gots.append(swap_dp(go, order[len(gots)]))
            if len(gots) == len(order):
                return go

    inputs = tokens.astype(F32)
    scale_one = lax.rsqrt(jnp.mean(inputs * inputs, axis=-1, keepdims=True) + EPSILON)
    normed = (inputs * scale_one * gain_attn).astype(BF)
    one = along(normed, PAIRS)
    near = along(normed, MIDDLE)
    w_qkv = jnp.concatenate([w_query, w_key, w_value], axis=1)
    qkv_0 = dot(normed, w_qkv).astype(BF)
    near, one = after(near, qkv_0), after(one, qkv_0)
    far = along(one, MIDDLE)
    two = exchange(near, out_cotangent)
    qkv_1 = dot(one, w_qkv).astype(BF)
    cot_near = along(after(out_cotangent, qkv_1), MIDDLE)
    far, two = after(far, qkv_1), after(two, qkv_1)
    three = along(far, OUTWARD)
    cot_1 = two
    slot_2 = jnp.where(is_middle, near, two)
    qkv_2 = dot(slot_2, w_qkv).astype(BF)
    cot_far = along(after(cot_1, slot_2), MIDDLE)
    three = after(three, qkv_2, cot_near)
    slot_3 = jnp.where(is_middle, far, three)
    qkv_3 = dot(slot_3, w_qkv).astype(BF)
    normed_full = jnp.concatenate([normed, one, slot_2, slot_3], axis=0)
    qkv = jnp.concatenate([qkv_0, qkv_1, qkv_2, qkv_3], axis=0)
    mixed = attention(places, bound, qkv)

    third = dot(rows_of(mixed, 3), w_out).astype(BF)
    edge = exchange(out_cotangent, third)
    second = dot(after(rows_of(mixed, 2), third), w_out).astype(BF)
    first = dot(after(rows_of(mixed, 1), third), w_out)
    zeroth = dot(after(rows_of(mixed, 0), third), w_out)
    edge = after(edge, second, first, zeroth)
    across = along(third + edge, MIDDLE)
    edge_two = exchange(cot_near, after(second, edge))
    cot_1 = jnp.where(is_middle, cot_1, edge)
    mixed_both = both_rows(after(mixed, edge))
    normed_blocks = column_blocks(after(normed_full, edge))
    across, edge_two, cot_far = (
        after(across, mixed_both, normed_blocks, cot_1),
        after(edge_two, mixed_both, normed_blocks, cot_1),
        after(cot_far, mixed_both, normed_blocks, cot_1),
    )
    pair = along((first + across.astype(F32)).astype(BF), PAIRS)
    middle = along(second + edge_two, MIDDLE)
    cot_2 = jnp.where(is_middle, cot_near, edge_two)
    cot_three = along(after(cot_far, cot_2), OUTWARD)
    back_012 = dot_nt(jnp.concatenate([out_cotangent, cot_1, cot_2], axis=0), w_down).astype(BF)
    pair, middle = after(pair, back_012), after(middle, back_012)
    resid = inputs + (zeroth + pair.astype(F32) + middle.astype(F32))

    scale_two = lax.rsqrt(jnp.mean(resid * resid, axis=-1, keepdims=True) + EPSILON)
    normed_two = (resid * scale_two * gain_mlp).astype(BF)

    def feed(slot_rows, back):
        gate = dot(slot_rows, w_gate)
        upward = dot(slot_rows, w_up)
        sig = jax.nn.sigmoid(gate)
        active = gate * sig
        back = back.astype(F32)
        hid = (active * upward).astype(BF)
        d_g = (back * upward * sig * (1.0 + gate * (1.0 - sig))).astype(BF)
        d_u = (back * active).astype(BF)
        return hid, d_g, d_u

    def unfeed(fed):
        return dot_nt(fed[1], w_gate) + dot_nt(fed[2], w_up)

    one = along(normed_two, PAIRS)
    near = along(normed_two, MIDDLE)
    fed_0 = feed(normed_two, rows_of(back_012, 0))
    part_0 = unfeed(fed_0)
    near, one = after(near, part_0), after(one, part_0)
    two = along(near, OUTWARD)
    far = along(one, MIDDLE)
    fed_1 = feed(one, rows_of(back_012, 1))
    part_1 = unfeed(fed_1)
    out_1 = dot(fed_1[0], w_down)
    cot_3 = jnp.where(is_middle, cot_far, after(cot_three, one))
    back_3 = dot_nt(cot_3, w_down).astype(BF)
    far, two = after(far, part_1, out_1, back_3), after(two, part_1, out_1, back_3)
    three = exchange(far, out_1.astype(BF))
    cot_full = jnp.concatenate([out_cotangent, cot_1, cot_2, after(cot_3, two)], axis=0)
    cot_columns = half_columns(cot_full)
    slot_2 = jnp.where(is_middle, near, two)
    fed_2 = feed(slot_2, rows_of(back_012, 2))
    part_2 = unfeed(fed_2).astype(BF)
    three = after(three, part_2, cot_columns)
    out_in = three
    slot_3 = jnp.where(is_middle, far, three)
    fed_3 = feed(slot_3, back_3)
    third = unfeed(fed_3).astype(BF)

    edge = along(third, INWARD)
    hidden_s, d_gate_s, d_up_s = zip(fed_0, fed_1, fed_2, fed_3)
    hidden_both = both_rows(after(jnp.concatenate(hidden_s, axis=0), third))
    second_full = jnp.concatenate([normed_two, one, slot_2, slot_3], axis=0)
    down_pay = [half_sums(cot_columns, hidden_both, side, 0, []).astype(BF) for side in (0, 1)]
    down_got = send_halves(down_pay, 0)
    edge = after(edge, *down_pay)
    across = along(third + edge, MIDDLE)
    edge_two = along(after(part_2, edge), INWARD)
    second_columns = half_columns(after(second_full, edge))
    d_feed = jnp.concatenate(
        [jnp.concatenate([g, u], axis=1) for g, u in zip(d_gate_s, d_up_s)], axis=0
    )
    feed_both = both_rows(after(d_feed, edge))
    feed_pay = [half_sums(second_columns, feed_both, side, 0, []).astype(BF) for side in (0, 1)]
    across, edge_two = after(across, *feed_pay), after(edge_two, *feed_pay)
    pair = along((part_1 + across.astype(F32)).astype(BF), PAIRS)
    middle = along(part_2 + edge_two, MIDDLE)
    down_got = [after(g, across) for g in down_got]
    feed_got = send_halves([after(p, *down_got) for p in feed_pay], 0)
    out_3 = dot(after(fed_3[0], across), w_down).astype(BF)
    pair = after(pair, out_3)
    d_normed_two = part_0 + pair.astype(F32) + middle.astype(F32)
    weighted_two = d_normed_two * gain_mlp
    d_resid = (
        out_cotangent.astype(F32)
        + scale_two * weighted_two
        - resid * scale_two**3 * jnp.mean(weighted_two * resid, axis=-1, keepdims=True)
    )
    d_attn = d_resid.astype(BF)

    one = along(d_attn, PAIRS)
    near = along(d_attn, MIDDLE)
    gain_two_part = jnp.sum(d_normed_two * resid * scale_two, axis=0)
    out_2 = dot(after(fed_2[0], d_attn), w_down).astype(BF)
    out_0 = dot(after(fed_0[0], d_attn), w_down)
    early = (gain_two_part, out_0, out_2)
    near, one = after(near, *early), after(one, *early)
    far = along(one, MIDDLE)
    two = exchange(near, out_3)
    d_mixed_0 = dot_nt(after(d_attn, one), w_out).astype(BF)
    d_mixed_1 = dot_nt(after(one, d_mixed_0), w_out).astype(BF)
    far, two = after(far, d_mixed_1), after(two, d_mixed_1)
    three = exchange(far, out_2)
    slot_2 = jnp.where(is_middle, near, two)
    d_mixed_2 = dot_nt(slot_2, w_out).astype(BF)
    out_across = along(out_3 + after(two, d_mixed_2), MIDDLE)
    before = attention_back(
        places, bound, qkv, jnp.concatenate([d_mixed_0, d_mixed_1, d_mixed_2], axis=0), 0, None
    )
    feed_got = [after(g, d_mixed_1) for g in feed_got]
    feed_gots = [[g] for g in feed_got]
    down_gots = [[g] for g in down_got]
    for stage in range(1, len(order_one)):
        rest = [
            jnp.concatenate(
                [
                    half_sums(second_columns, feed_both, side, stage, feed_gots[side]),
                    half_sums(cot_columns, hidden_both, side, stage, down_gots[side]),
                ],
                axis=1,
            ).astype(BF)
            for side in (0, 1)
        ]
        for side, got in enumerate(send_halves(rest, stage)):
            got = after(got, before[0])
            feed_gots[side].append(got[:, : d_feed.shape[1]])
            down_gots[side].append(got[:, d_feed.shape[1] :])
    rest_got = got
    three = after(three, before[0])
    slot_3 = jnp.where(is_middle, far, three)
    d_mixed_3 = dot_nt(slot_3, w_out).astype(BF)
    d_qkv = attention_back(places, bound, qkv, d_mixed_3, 3 * shard, before)

    third = dot_nt(rows_of(d_qkv, 3), w_qkv).astype(BF)
    edge = along(third, INWARD)
    qkv_both = both_rows(after(d_qkv, third))
    second = dot_nt(after(rows_of(d_qkv, 2), third), w_qkv).astype(BF)
    first = dot_nt(after(rows_of(d_qkv, 1), third), w_qkv)
    zeroth = dot_nt(after(rows_of(d_qkv, 0), third), w_qkv)
    out_middle = along(after(out_2 + three, second), MIDDLE)
    out_sum = (out_1 + after(out_across, second).astype(F32)).astype(BF)
    d_normed_part = jnp.concatenate([zeroth, first, second.astype(F32), third.astype(F32)], axis=0)
    gain_one_part = jnp.sum(d_normed_part * normed_full.astype(F32), axis=0)
    gains = jnp.stack([gain_one_part / gain_attn, gain_two_part])
    gains = gains + swap_dp(gains, bits[0])
    gains_got = swap_dp(gains, bits[1])
    of_qkv = (normed_blocks, after(qkv_both, gains), 0, order_one)
    qkv_go = block_sums(*of_qkv, []).astype(BF)
    qkv_got = swap_dp(qkv_go, order_one[0])
    edge = after(edge, out_sum, gains, rest_got)
    across = along(third + edge, MIDDLE)
    edge_two = exchange(out_sum, after(second, edge))
    gains = gains + after(gains_got, edge)
    for bit in bits[2:]:
        gains = gains + swap_dp(gains, bit)
    attn_full = jnp.concatenate([d_attn, one, slot_2, slot_3], axis=0)
    attn_blocks = column_blocks(after(attn_full, edge))
    of_out = (after(attn_blocks, gains_got), mixed_both, 1, order_two)
    out_go = block_sums(*of_out, []).astype(BF)
    out_got = swap_dp(out_go, order_two[0])
    across, edge_two = after(across, gains), after(edge_two, gains)
    grad_down = final_rows(after(cot_columns, edge), hidden_both, down_gots).T
    gains = gains.astype(BF)
    pair = along(
        jnp.concatenate([(first + across.astype(F32)).astype(BF), gains], axis=0), PAIRS
    )
    middle = along(second + edge_two, MIDDLE)
    qkv_gots = [after(qkv_got, across)]
    qkv_mid = pass_on(of_qkv, qkv_gots)
    grad_feed = final_rows(after(second_columns, edge), feed_both, feed_gots)
    out_gots = [after(out_got, across)]
    out_back = pass_on(of_out, out_gots)
    gains = gains.astype(F32) + pair[shard:].astype(F32)
    gains = gains + along(gains, [(i, i ^ 2) for i in range(4)])
    pair = pair[:shard]
    grad_qkv = block_sums(*of_qkv, qkv_gots)
    grad_out = block_sums(*of_out, out_gots)
    out_rest = jnp.where(
        is_middle, out_in.astype(F32) + after(out_middle, across).astype(F32), edge_two.astype(F32)
    )
    outputs = (resid + (out_0 + out_rest)).astype(BF)
    d_normed = zeroth + pair.astype(F32) + middle.astype(F32)
    weighted_one = d_normed * gain_attn
    grad_tokens = (
        d_resid
        + scale_one * weighted_one
        - inputs * scale_one**3 * jnp.mean(weighted_one * inputs, axis=-1, keepdims=True)
    )
    return (
        outputs,
        grad_tokens,
        grad_qkv[:, :n_q],
        grad_qkv[:, n_q : 2 * n_q],
        grad_qkv[:, 2 * n_q :],
        grad_out,
        grad_feed[:, : w_gate.shape[1]],
        grad_feed[:, w_gate.shape[1] :],
        grad_down,
        gains[0],
        gains[1],
    )


def solution(mesh):
    return jax.shard_map(
        on_device,
        mesh=mesh,
        in_specs=(
            P(("dp", "mp"), None),
            P("dp"),
            P(None, "mp"),
            P(None, "mp"),
            P(None, "mp"),
            P("mp", None),
            P(None, "mp"),
            P(None, "mp"),
            P("mp", None),
            P(),
            P(),
            P(("dp", "mp"), None),
        ),
        out_specs=(
            P(("dp", "mp"), None),
            P(("dp", "mp"), None),
            P("dp", "mp"),
            P("dp", "mp"),
            P("dp", "mp"),
            P("mp", "dp"),
            P("dp", "mp"),
            P("dp", "mp"),
            P("mp", "dp"),
            P(),
            P(),
        ),
        check_vma=False,
    )
```

```python
import functools

import jax
import jax.numpy as jnp
from jax import lax
from jax.experimental import pallas as pl
from jax.experimental.pallas import tpu as pltpu
from jax.sharding import PartitionSpec as P

FK = 16
DV = 128
BF = jnp.bfloat16
F32 = jnp.float32
EPSILON = 1e-06
BLOCK = 128
UNSEEN = 1 << 24
LANES = 128

PAIRS = [(0, 1), (1, 0), (2, 3), (3, 2)]
MIDDLE = [(1, 2), (2, 1)]
OUTWARD = [(2, 3), (1, 0)]
INWARD = [(3, 2), (0, 1)]


def dot(left, right):
    return jnp.dot(left, right, preferred_element_type=F32)


def dot_nt(left, right):
    return lax.dot_general(left, right, (((1,), (1,)), ((), ())), preferred_element_type=F32)


def dot_tn(left, right):
    return lax.dot_general(left, right, (((0,), (0,)), ((), ())), preferred_element_type=F32)


def head_lanes(array, head):
    lane = lax.broadcasted_iota(jnp.int32, array.shape, 1) // FK
    return jnp.where(lane == head, array.astype(F32), 0.0).astype(BF)


def weights_of(query, key, seen):
    inner = dot_nt(query, key)
    weight = jnp.where(seen, 1.0 + inner * (0.25 + inner * (1.0 / 32.0)), 0.0)
    return inner, weight, 1.0 / jnp.sum(weight, axis=-1, keepdims=True)


def attention_kernel(heads, place_ref, bound_ref, qkv_ref, mixed_ref):
    n_q = heads * FK
    key = qkv_ref[:, n_q : 2 * n_q]
    queries = [head_lanes(qkv_ref[:, :n_q], h) for h in range(heads)]
    bound = bound_ref[...]
    for first in range(0, qkv_ref.shape[0], BLOCK):
        seen = bound <= place_ref[first : first + BLOCK]
        for h in range(heads):
            _, weight, scale = weights_of(queries[h][first : first + BLOCK], key, seen)
            value = qkv_ref[:, 2 * n_q + h * DV : 2 * n_q + (h + 1) * DV]
            mixed_ref[first : first + BLOCK, h * DV : (h + 1) * DV] = dot(
                (weight * scale).astype(BF), value
            ).astype(BF)


def cost(flops):
    return pl.CostEstimate(flops=flops, bytes_accessed=2**21, transcendentals=0)


def attention(place, bound, qkv):
    heads = (qkv.shape[1] // (2 * FK + DV))
    return pl.pallas_call(
        functools.partial(attention_kernel, heads),
        out_shape=jax.ShapeDtypeStruct((qkv.shape[0], heads * DV), BF),
        compiler_params=pltpu.CompilerParams(vmem_limit_bytes=32 * 2**20),
        cost_estimate=cost(qkv.shape[0] * qkv.shape[0] * heads * 2 * (2 * FK + DV) * 16),
        name="attention",
    )(place, bound, qkv)


def attention_back_kernel(heads, start, last, *refs):
    if last:
        place_ref, bound_ref, qkv_ref, d_mixed_ref, query_ref, total_ref, out_ref = refs
    else:
        place_ref, bound_ref, qkv_ref, d_mixed_ref, query_ref, total_ref = refs
    n_q = heads * FK
    key = qkv_ref[:, n_q : 2 * n_q]
    keys = [head_lanes(key, h) for h in range(heads)]
    bound = bound_ref[...]
    rows = d_mixed_ref.shape[0]
    d_key = 0.0
    d_values = [0.0] * heads
    for first in range(0, rows, BLOCK):
        here = slice(start + first, start + first + BLOCK)
        seen = bound <= place_ref[here]
        d_query = 0.0
        for h in range(heads):
            query = head_lanes(qkv_ref[here, :n_q], h)
            inner, weight, scale = weights_of(query, key, seen)
            share = weight * scale
            value = qkv_ref[:, 2 * n_q + h * DV : 2 * n_q + (h + 1) * DV]
            d_out = d_mixed_ref[first : first + BLOCK, h * DV : (h + 1) * DV]
            d_share = dot_nt(d_out, value)
            row = jnp.sum(d_share * share, axis=-1, keepdims=True)
            d_inner = jnp.where(
                seen, (d_share - row) * scale * (0.25 + inner * (1.0 / 16.0)), 0.0
            ).astype(BF)
            d_query = d_query + dot(d_inner, keys[h])
            d_key = d_key + dot_tn(d_inner, query)
            d_values[h] = d_values[h] + dot_tn(share.astype(BF), d_out)
        if last:
            out_ref[here, :n_q] = d_query.astype(BF)
        else:
            query_ref[first : first + BLOCK] = d_query.astype(BF)
    if last:
        out_ref[:start, :n_q] = query_ref[...]
        out_ref[:, n_q : 2 * n_q] = (d_key + total_ref[:, heads * DV :]).astype(BF)
        for h in range(heads):
            out_ref[:, 2 * n_q + h * DV : 2 * n_q + (h + 1) * DV] = (
                d_values[h] + total_ref[:, h * DV : (h + 1) * DV]
            ).astype(BF)
    else:
        total_ref[:, heads * DV :] = d_key
        for h in range(heads):
            total_ref[:, h * DV : (h + 1) * DV] = d_values[h]


def attention_back(place, bound, qkv, d_mixed, start, before):
    heads = (qkv.shape[1] // (2 * FK + DV))
    n_q = heads * FK
    rows = d_mixed.shape[0]
    last = before is not None
    if last:
        shape = jax.ShapeDtypeStruct(qkv.shape, BF)
    else:
        shape = (
            jax.ShapeDtypeStruct((rows, n_q), BF),
            jax.ShapeDtypeStruct((qkv.shape[0], n_q + heads * DV), F32),
        )
    return pl.pallas_call(
        functools.partial(attention_back_kernel, heads, start, last),
        out_shape=shape,
        compiler_params=pltpu.CompilerParams(vmem_limit_bytes=40 * 2**20),
        cost_estimate=cost(rows * qkv.shape[0] * heads * 2 * (6 * FK + 2 * DV)),
        name="attention_back",
    )(place, bound, qkv, d_mixed, *(before or ()))


def after(value, *others):
    return lax.optimization_barrier((value, *others))[0]


def along(value, pairs):
    return lax.ppermute(value, "mp", pairs)


def on_device(
    tokens,
    lengths,
    w_query,
    w_key,
    w_value,
    w_out,
    w_gate,
    w_up,
    w_down,
    gain_attn,
    gain_mlp,
    out_cotangent,
):
    shard = tokens.shape[0]
    width = tokens.shape[1]
    heads = w_query.shape[1] // FK
    n_q = w_query.shape[1]
    n_dp = lax.axis_size("dp")
    block = width // n_dp
    bits = [1 << b for b in range(n_dp.bit_length() - 1)]
    me_mp = lax.axis_index("mp")
    me_dp = lax.axis_index("dp")
    is_middle = (me_mp == 1) | (me_mp == 2)
    chunk_ids = [
        me_mp,
        me_mp ^ 1,
        jnp.where(is_middle, me_mp ^ 3, me_mp ^ 2),
        jnp.where(is_middle, me_mp ^ 2, me_mp ^ 3),
    ]
    places = jnp.concatenate([c * shard + jnp.arange(shard, dtype=jnp.int32) for c in chunk_ids])
    bound = jnp.where(places < lengths[0], places, UNSEEN)[None, :]
    places = places[:, None]

    order_one = bits[1:]
    order_two = order_one[::-1]
    even_slots = [2, 6, 4, 0] if n_dp == 8 else list(range(0, n_dp, 2))
    second_slots = [0, 2, 6, 4] if n_dp == 8 else list(range(0, n_dp, 2))

    def rows_of(array, slot):
        return array[slot * shard : (slot + 1) * shard]

    def exchange(outward, inward):
        return along(jnp.where(is_middle, outward, inward), PAIRS)

    def swap_dp(value, bit):
        return lax.ppermute(value, "dp", [(i, i ^ bit) for i in range(n_dp)])

    def both_rows(array):
        return jnp.concatenate([array, swap_dp(array, 1)], axis=0)

    def take(array, held, slots, axis, size=None):
        size = size or block
        at = [held.index(k) for k in slots]
        if at == list(range(at[0], at[0] + len(at))):
            return lax.slice_in_dim(array, at[0] * size, (at[-1] + 1) * size, axis=axis)
        return jnp.concatenate(
            [lax.slice_in_dim(array, i * size, (i + 1) * size, axis=axis) for i in at], axis=axis
        )

    def column_blocks(array):
        def pick(slots):
            return jnp.concatenate(
                [
                    lax.dynamic_slice_in_dim(array, (me_dp ^ k) * block, block, axis=1)
                    for k in slots
                ],
                axis=1,
            )

        theirs = swap_dp(pick([k ^ 1 for k in even_slots]), 1)
        return jnp.concatenate([pick(even_slots), theirs], axis=0)

    half = block // 2

    def half_columns(array):
        def pick(odd):
            cuts = [(k, 0) for k in even_slots] + [(k, half) for k in second_slots]
            return jnp.concatenate(
                [
                    lax.dynamic_slice_in_dim(
                        array, (me_dp ^ k ^ odd) * block + shift, half, axis=1
                    )
                    for k, shift in cuts
                ],
                axis=1,
            )

        joined = jnp.concatenate([pick(0), swap_dp(pick(1), 1)], axis=0)
        return joined

    def half_sums(columns, other, side, stage, gots):
        order = (order_one, order_two)[side]
        held = (even_slots, second_slots)[side]
        base = side * len(even_slots) * half
        cut = lax.slice_in_dim(columns, base, base + len(even_slots) * half, axis=1)
        slots = away_slots(order, stage)
        total = dot_tn(take(cut, held, slots, 1, half), other)
        for earlier, got in enumerate(gots):
            there = [k ^ order[earlier] for k in away_slots(order, earlier)]
            total = total + take(got, there, slots, 0, half).astype(F32)
        return total

    def send_halves(pair_of_halves, stage):
        return [
            swap_dp(part, order[stage])
            for part, order in zip(pair_of_halves, (order_one, order_two))
        ]

    def final_rows(columns, other, gots):
        last = len(order_one)
        if even_slots[-1] == second_slots[0] == 0:
            at = (len(even_slots) - 1) * half
            total = dot_tn(lax.slice_in_dim(columns, at, at + block, axis=1), other)
            parts = [total[:half], total[half:]]
            for side, order in enumerate((order_one, order_two)):
                for stage, got in enumerate(gots[side]):
                    there = [k ^ order[stage] for k in away_slots(order, stage)]
                    parts[side] = parts[side] + take(got, there, [0], 0, half).astype(F32)
        else:
            parts = [half_sums(columns, other, side, last, gots[side]) for side in (0, 1)]
        return jnp.concatenate(parts, axis=0)

    def away_slots(order, stage):
        if stage == len(order):
            return [0]
        return [
            k for k in even_slots if k & order[stage] and not any(k & b for b in order[:stage])
        ]

    def block_sums(blocks, other, axis, order, gots):
        slots = away_slots(order, len(gots))
        picked = take(blocks, even_slots, slots, 1)
        total = dot_tn(picked, other) if axis == 0 else dot_tn(other, picked)
        for stage, got in enumerate(gots):
            held = [k ^ order[stage] for k in away_slots(order, stage)]
            total = total + take(got, held, slots, axis).astype(F32)
        return total

    def pass_on(sums, gots):
        blocks, other, axis, order = sums
        while True:
            go = block_sums(*sums, gots).astype(BF)
            gots.append(swap_dp(go, order[len(gots)]))
            if len(gots) == len(order):
                return go

    inputs = tokens.astype(F32)
    scale_one = lax.rsqrt(jnp.mean(inputs * inputs, axis=-1, keepdims=True) + EPSILON)
    normed = (inputs * scale_one * gain_attn).astype(BF)
    one = along(normed, PAIRS)
    near = along(normed, MIDDLE)
    w_qkv = jnp.concatenate([w_query, w_key, w_value], axis=1)
    qkv_0 = dot(normed, w_qkv).astype(BF)
    near, one = after(near, qkv_0), after(one, qkv_0)
    far = along(one, MIDDLE)
    two = exchange(near, out_cotangent)
    qkv_1 = dot(one, w_qkv).astype(BF)
    cot_near = along(after(out_cotangent, qkv_1), MIDDLE)
    far, two = after(far, qkv_1), after(two, qkv_1)
    three = along(far, OUTWARD)
    cot_1 = two
    slot_2 = jnp.where(is_middle, near, two)
    qkv_2 = dot(slot_2, w_qkv).astype(BF)
    cot_far = along(after(cot_1, slot_2), MIDDLE)
    three = after(three, qkv_2, cot_near)
    slot_3 = jnp.where(is_middle, far, three)
    qkv_3 = dot(slot_3, w_qkv).astype(BF)
    normed_full = jnp.concatenate([normed, one, slot_2, slot_3], axis=0)
    qkv = jnp.concatenate([qkv_0, qkv_1, qkv_2, qkv_3], axis=0)
    mixed = attention(places, bound, qkv)

    third = dot(rows_of(mixed, 3), w_out).astype(BF)
    edge = exchange(out_cotangent, third)
    second = dot(after(rows_of(mixed, 2), third), w_out).astype(BF)
    first = dot(after(rows_of(mixed, 1), third), w_out)
    zeroth = dot(after(rows_of(mixed, 0), third), w_out)
    edge = after(edge, second, first, zeroth)
    across = along(third + edge, MIDDLE)
    edge_two = exchange(cot_near, after(second, edge))
    cot_1 = jnp.where(is_middle, cot_1, edge)
    mixed_both = both_rows(after(mixed, edge))
    normed_blocks = column_blocks(after(normed_full, edge))
    across, edge_two, cot_far = (
        after(across, mixed_both, normed_blocks, cot_1),
        after(edge_two, mixed_both, normed_blocks, cot_1),
        after(cot_far, mixed_both, normed_blocks, cot_1),
    )
    pair = along((first + across.astype(F32)).astype(BF), PAIRS)
    middle = along(second + edge_two, MIDDLE)
    cot_2 = jnp.where(is_middle, cot_near, edge_two)
    cot_three = along(after(cot_far, cot_2), OUTWARD)
    back_012 = dot_nt(jnp.concatenate([out_cotangent, cot_1, cot_2], axis=0), w_down).astype(BF)
    pair, middle = after(pair, back_012), after(middle, back_012)
    resid = inputs + (zeroth + pair.astype(F32) + middle.astype(F32))

    scale_two = lax.rsqrt(jnp.mean(resid * resid, axis=-1, keepdims=True) + EPSILON)
    normed_two = (resid * scale_two * gain_mlp).astype(BF)

    units = w_gate.shape[1]
    wide = -(-units // LANES) * LANES

    def feed(slot_rows, back):
        gate = dot(slot_rows, w_gate)
        upward = dot(slot_rows, w_up)
        sig = jax.nn.sigmoid(gate)
        active = gate * sig
        back = back.astype(F32)
        hid = (active * upward).astype(BF)
        d_g = (back * upward * sig * (1.0 + gate * (1.0 - sig))).astype(BF)
        d_u = (back * active).astype(BF)
        d_g, d_u = (jnp.pad(d, ((0, 0), (0, wide - units))) for d in (d_g, d_u))
        return hid, d_g, d_u

    def unfeed(fed):
        return dot_nt(fed[1][:, :units], w_gate) + dot_nt(fed[2][:, :units], w_up)

    one = along(normed_two, PAIRS)
    near = along(normed_two, MIDDLE)
    fed_0 = feed(normed_two, rows_of(back_012, 0))
    part_0 = unfeed(fed_0)
    near, one = after(near, part_0), after(one, part_0)
    two = along(near, OUTWARD)
    far = along(one, MIDDLE)
    fed_1 = feed(one, rows_of(back_012, 1))
    part_1 = unfeed(fed_1)
    out_1 = dot(fed_1[0], w_down)
    cot_3 = jnp.where(is_middle, cot_far, after(cot_three, one))
    back_3 = dot_nt(cot_3, w_down).astype(BF)
    far, two = after(far, part_1, out_1, back_3), after(two, part_1, out_1, back_3)
    three = exchange(far, out_1.astype(BF))
    cot_full = jnp.concatenate([out_cotangent, cot_1, cot_2, after(cot_3, two)], axis=0)
    cot_columns = half_columns(cot_full)
    slot_2 = jnp.where(is_middle, near, two)
    fed_2 = feed(slot_2, rows_of(back_012, 2))
    part_2 = unfeed(fed_2).astype(BF)
    three = after(three, part_2, cot_columns)
    out_in = three
    slot_3 = jnp.where(is_middle, far, three)
    fed_3 = feed(slot_3, back_3)
    third = unfeed(fed_3).astype(BF)

    edge = along(third, INWARD)
    hidden_s, d_gate_s, d_up_s = zip(fed_0, fed_1, fed_2, fed_3)
    hidden_both = both_rows(after(jnp.concatenate(hidden_s, axis=0), third))
    second_full = jnp.concatenate([normed_two, one, slot_2, slot_3], axis=0)
    down_pay = [half_sums(cot_columns, hidden_both, side, 0, []).astype(BF) for side in (0, 1)]
    down_got = send_halves(down_pay, 0)
    edge = after(edge, *down_pay)
    across = along(third + edge, MIDDLE)
    edge_two = along(after(part_2, edge), INWARD)
    second_columns = half_columns(after(second_full, edge))
    d_feed = jnp.concatenate(
        [jnp.concatenate([g, u], axis=1) for g, u in zip(d_gate_s, d_up_s)], axis=0
    )
    feed_both = both_rows(after(d_feed, edge))
    feed_pay = [half_sums(second_columns, feed_both, side, 0, []).astype(BF) for side in (0, 1)]
    across, edge_two = after(across, *feed_pay), after(edge_two, *feed_pay)
    pair = along((part_1 + across.astype(F32)).astype(BF), PAIRS)
    middle = along(part_2 + edge_two, MIDDLE)
    down_got = [after(g, across) for g in down_got]
    feed_got = send_halves([after(p, *down_got) for p in feed_pay], 0)
    out_3 = dot(after(fed_3[0], across), w_down).astype(BF)
    pair = after(pair, out_3)
    d_normed_two = part_0 + pair.astype(F32) + middle.astype(F32)
    weighted_two = d_normed_two * gain_mlp
    d_resid = (
        out_cotangent.astype(F32)
        + scale_two * weighted_two
        - resid * scale_two**3 * jnp.mean(weighted_two * resid, axis=-1, keepdims=True)
    )
    d_attn = d_resid.astype(BF)

    one = along(d_attn, PAIRS)
    near = along(d_attn, MIDDLE)
    gain_two_part = jnp.sum(d_normed_two * resid * scale_two, axis=0)
    out_2 = dot(after(fed_2[0], d_attn), w_down).astype(BF)
    out_0 = dot(after(fed_0[0], d_attn), w_down)
    early = (gain_two_part, out_0, out_2)
    near, one = after(near, *early), after(one, *early)
    far = along(one, MIDDLE)
    two = exchange(near, out_3)
    d_mixed_0 = dot_nt(after(d_attn, one), w_out).astype(BF)
    d_mixed_1 = dot_nt(after(one, d_mixed_0), w_out).astype(BF)
    far, two = after(far, d_mixed_1), after(two, d_mixed_1)
    three = exchange(far, out_2)
    slot_2 = jnp.where(is_middle, near, two)
    d_mixed_2 = dot_nt(slot_2, w_out).astype(BF)
    out_across = along(out_3 + after(two, d_mixed_2), MIDDLE)
    before = attention_back(
        places, bound, qkv, jnp.concatenate([d_mixed_0, d_mixed_1, d_mixed_2], axis=0), 0, None
    )
    feed_got = [after(g, d_mixed_1) for g in feed_got]
    feed_gots = [[g] for g in feed_got]
    down_gots = [[g] for g in down_got]
    for stage in range(1, len(order_one)):
        rest = [
            jnp.concatenate(
                [
                    half_sums(second_columns, feed_both, side, stage, feed_gots[side]),
                    half_sums(cot_columns, hidden_both, side, stage, down_gots[side]),
                ],
                axis=1,
            ).astype(BF)
            for side in (0, 1)
        ]
        for side, got in enumerate(send_halves(rest, stage)):
            got = after(got, before[0])
            feed_gots[side].append(got[:, : d_feed.shape[1]])
            down_gots[side].append(got[:, d_feed.shape[1] :])
    rest_got = got
    three = after(three, before[0])
    slot_3 = jnp.where(is_middle, far, three)
    d_mixed_3 = dot_nt(slot_3, w_out).astype(BF)
    d_qkv = attention_back(places, bound, qkv, d_mixed_3, 3 * shard, before)

    third = dot_nt(rows_of(d_qkv, 3), w_qkv).astype(BF)
    edge = along(third, INWARD)
    qkv_both = both_rows(after(d_qkv, third))
    second = dot_nt(after(rows_of(d_qkv, 2), third), w_qkv).astype(BF)
    first = dot_nt(after(rows_of(d_qkv, 1), third), w_qkv)
    zeroth = dot_nt(after(rows_of(d_qkv, 0), third), w_qkv)
    out_middle = along(after(out_2 + three, second), MIDDLE)
    out_sum = (out_1 + after(out_across, second).astype(F32)).astype(BF)
    d_normed_part = jnp.concatenate([zeroth, first, second.astype(F32), third.astype(F32)], axis=0)
    gain_one_part = jnp.sum(d_normed_part * normed_full.astype(F32), axis=0)
    gains = jnp.stack([gain_one_part / gain_attn, gain_two_part])
    gains = gains + swap_dp(gains, bits[0])
    gains_got = swap_dp(gains, bits[1])
    of_qkv = (normed_blocks, after(qkv_both, gains), 0, order_one)
    qkv_go = block_sums(*of_qkv, []).astype(BF)
    qkv_got = swap_dp(qkv_go, order_one[0])
    edge = after(edge, out_sum, gains, rest_got)
    across = along(third + edge, MIDDLE)
    edge_two = exchange(out_sum, after(second, edge))
    gains = gains + after(gains_got, edge)
    for bit in bits[2:]:
        gains = gains + swap_dp(gains, bit)
    attn_full = jnp.concatenate([d_attn, one, slot_2, slot_3], axis=0)
    attn_blocks = column_blocks(after(attn_full, third))
    of_out = (attn_blocks, mixed_both, 1, order_two)
    out_go = block_sums(*of_out, []).astype(BF)
    out_got = swap_dp(out_go, order_two[0])
    across, edge_two = after(across, gains), after(edge_two, gains)
    gains = gains.astype(BF)
    pair = along(
        jnp.concatenate([(first + across.astype(F32)).astype(BF), gains], axis=0), PAIRS
    )
    middle = along(second + edge_two, MIDDLE)
    qkv_gots = [after(qkv_got, across)]
    qkv_mid = pass_on(of_qkv, qkv_gots)
    out_gots = [after(out_got, across)]
    out_back = pass_on(of_out, out_gots)
    gains = gains.astype(F32) + pair[shard:].astype(F32)
    gains = gains + along(gains, [(i, i ^ 2) for i in range(4)])
    pair = pair[:shard]
    grad_down = final_rows(after(cot_columns, qkv_mid), hidden_both, down_gots).T
    grad_feed = final_rows(after(second_columns, pair), feed_both, feed_gots)
    grad_qkv = block_sums(*of_qkv, qkv_gots)
    grad_out = block_sums(*of_out, out_gots)
    out_rest = jnp.where(
        is_middle, out_in.astype(F32) + after(out_middle, across).astype(F32), edge_two.astype(F32)
    )
    outputs = (resid + (out_0 + out_rest)).astype(BF)
    d_normed = zeroth + pair.astype(F32) + middle.astype(F32)
    weighted_one = d_normed * gain_attn
    grad_tokens = (
        d_resid
        + scale_one * weighted_one
        - inputs * scale_one**3 * jnp.mean(weighted_one * inputs, axis=-1, keepdims=True)
    )
    return (
        outputs,
        grad_tokens,
        grad_qkv[:, :n_q],
        grad_qkv[:, n_q : 2 * n_q],
        grad_qkv[:, 2 * n_q :],
        grad_out,
        grad_feed[:, :units],
        grad_feed[:, wide : wide + units],
        grad_down,
        gains[0],
        gains[1],
    )


def solution(mesh):
    return jax.shard_map(
        on_device,
        mesh=mesh,
        in_specs=(
            P(("dp", "mp"), None),
            P("dp"),
            P(None, "mp"),
            P(None, "mp"),
            P(None, "mp"),
            P("mp", None),
            P(None, "mp"),
            P(None, "mp"),
            P("mp", None),
            P(),
            P(),
            P(("dp", "mp"), None),
        ),
        out_specs=(
            P(("dp", "mp"), None),
            P(("dp", "mp"), None),
            P("dp", "mp"),
            P("dp", "mp"),
            P("dp", "mp"),
            P("mp", "dp"),
            P("dp", "mp"),
            P("dp", "mp"),
            P("mp", "dp"),
            P(),
            P(),
        ),
        check_vma=False,
    )
```

```python
import functools

import jax
import jax.numpy as jnp
from jax import lax
from jax.experimental import pallas as pl
from jax.experimental.pallas import tpu as pltpu
from jax.sharding import PartitionSpec as P

FK = 16
DV = 128
BF = jnp.bfloat16
F32 = jnp.float32
EPSILON = 1e-06
BLOCK = 128
UNSEEN = 1 << 24
LANES = 128

PAIRS = [(0, 1), (1, 0), (2, 3), (3, 2)]
MIDDLE = [(1, 2), (2, 1)]
OUTWARD = [(2, 3), (1, 0)]
INWARD = [(3, 2), (0, 1)]


def dot(left, right):
    return jnp.dot(left, right, preferred_element_type=F32)


def dot_nt(left, right):
    return lax.dot_general(left, right, (((1,), (1,)), ((), ())), preferred_element_type=F32)


def dot_tn(left, right):
    return lax.dot_general(left, right, (((0,), (0,)), ((), ())), preferred_element_type=F32)


def head_lanes(array, head):
    lane = lax.broadcasted_iota(jnp.int32, array.shape, 1) // FK
    return jnp.where(lane == head, array.astype(F32), 0.0).astype(BF)


def weights_of(query, key, seen):
    inner = dot_nt(query, key)
    weight = jnp.where(seen, 1.0 + inner * (0.25 + inner * (1.0 / 32.0)), 0.0)
    return inner, weight, 1.0 / jnp.sum(weight, axis=-1, keepdims=True)


def attention_kernel(heads, place_ref, bound_ref, qkv_ref, mixed_ref):
    n_q = heads * FK
    key = qkv_ref[:, n_q : 2 * n_q]
    queries = [head_lanes(qkv_ref[:, :n_q], h) for h in range(heads)]
    bound = bound_ref[...]
    for first in range(0, qkv_ref.shape[0], BLOCK):
        seen = bound <= place_ref[first : first + BLOCK]
        for h in range(heads):
            _, weight, scale = weights_of(queries[h][first : first + BLOCK], key, seen)
            value = qkv_ref[:, 2 * n_q + h * DV : 2 * n_q + (h + 1) * DV]
            mixed_ref[first : first + BLOCK, h * DV : (h + 1) * DV] = dot(
                (weight * scale).astype(BF), value
            ).astype(BF)


def cost(flops):
    return pl.CostEstimate(flops=flops, bytes_accessed=2**21, transcendentals=0)


def attention(place, bound, qkv):
    heads = (qkv.shape[1] // (2 * FK + DV))
    return pl.pallas_call(
        functools.partial(attention_kernel, heads),
        out_shape=jax.ShapeDtypeStruct((qkv.shape[0], heads * DV), BF),
        compiler_params=pltpu.CompilerParams(vmem_limit_bytes=32 * 2**20),
        cost_estimate=cost(qkv.shape[0] * qkv.shape[0] * heads * 2 * (2 * FK + DV) * 16),
        name="attention",
    )(place, bound, qkv)


def attention_back_kernel(heads, start, last, *refs):
    if last:
        place_ref, bound_ref, qkv_ref, d_mixed_ref, query_ref, total_ref, out_ref = refs
    else:
        place_ref, bound_ref, qkv_ref, d_mixed_ref, query_ref, total_ref = refs
    n_q = heads * FK
    key = qkv_ref[:, n_q : 2 * n_q]
    keys = [head_lanes(key, h) for h in range(heads)]
    bound = bound_ref[...]
    rows = d_mixed_ref.shape[0]
    d_key = 0.0
    d_values = [0.0] * heads
    for first in range(0, rows, BLOCK):
        here = slice(start + first, start + first + BLOCK)
        seen = bound <= place_ref[here]
        d_query = 0.0
        for h in range(heads):
            query = head_lanes(qkv_ref[here, :n_q], h)
            inner, weight, scale = weights_of(query, key, seen)
            share = weight * scale
            value = qkv_ref[:, 2 * n_q + h * DV : 2 * n_q + (h + 1) * DV]
            d_out = d_mixed_ref[first : first + BLOCK, h * DV : (h + 1) * DV]
            d_share = dot_nt(d_out, value)
            row = jnp.sum(d_share * share, axis=-1, keepdims=True)
            d_inner = jnp.where(
                seen, (d_share - row) * scale * (0.25 + inner * (1.0 / 16.0)), 0.0
            ).astype(BF)
            d_query = d_query + dot(d_inner, keys[h])
            d_key = d_key + dot_tn(d_inner, query)
            d_values[h] = d_values[h] + dot_tn(share.astype(BF), d_out)
        if last:
            out_ref[here, :n_q] = d_query.astype(BF)
        else:
            query_ref[first : first + BLOCK] = d_query.astype(BF)
    if last:
        out_ref[:start, :n_q] = query_ref[...]
        out_ref[:, n_q : 2 * n_q] = (d_key + total_ref[:, heads * DV :]).astype(BF)
        for h in range(heads):
            out_ref[:, 2 * n_q + h * DV : 2 * n_q + (h + 1) * DV] = (
                d_values[h] + total_ref[:, h * DV : (h + 1) * DV]
            ).astype(BF)
    else:
        total_ref[:, heads * DV :] = d_key
        for h in range(heads):
            total_ref[:, h * DV : (h + 1) * DV] = d_values[h]


def attention_back(place, bound, qkv, d_mixed, start, before):
    heads = (qkv.shape[1] // (2 * FK + DV))
    n_q = heads * FK
    rows = d_mixed.shape[0]
    last = before is not None
    if last:
        shape = jax.ShapeDtypeStruct(qkv.shape, BF)
    else:
        shape = (
            jax.ShapeDtypeStruct((rows, n_q), BF),
            jax.ShapeDtypeStruct((qkv.shape[0], n_q + heads * DV), F32),
        )
    return pl.pallas_call(
        functools.partial(attention_back_kernel, heads, start, last),
        out_shape=shape,
        compiler_params=pltpu.CompilerParams(vmem_limit_bytes=40 * 2**20),
        cost_estimate=cost(rows * qkv.shape[0] * heads * 2 * (6 * FK + 2 * DV)),
        name="attention_back",
    )(place, bound, qkv, d_mixed, *(before or ()))


def after(value, *others):
    return lax.optimization_barrier((value, *others))[0]


def along(value, pairs):
    return lax.ppermute(value, "mp", pairs)


def on_device(
    tokens,
    lengths,
    w_query,
    w_key,
    w_value,
    w_out,
    w_gate,
    w_up,
    w_down,
    gain_attn,
    gain_mlp,
    out_cotangent,
):
    shard = tokens.shape[0]
    width = tokens.shape[1]
    heads = w_query.shape[1] // FK
    n_q = w_query.shape[1]
    n_dp = lax.axis_size("dp")
    block = width // n_dp
    bits = [1 << b for b in range(n_dp.bit_length() - 1)]
    me_mp = lax.axis_index("mp")
    me_dp = lax.axis_index("dp")
    is_middle = (me_mp == 1) | (me_mp == 2)
    chunk_ids = [
        me_mp,
        me_mp ^ 1,
        jnp.where(is_middle, me_mp ^ 3, me_mp ^ 2),
        jnp.where(is_middle, me_mp ^ 2, me_mp ^ 3),
    ]
    places = jnp.concatenate([c * shard + jnp.arange(shard, dtype=jnp.int32) for c in chunk_ids])
    bound = jnp.where(places < lengths[0], places, UNSEEN)[None, :]
    places = places[:, None]

    order_one = bits[1:]
    order_two = order_one[::-1]
    even_slots = [2, 6, 4, 0] if n_dp == 8 else list(range(0, n_dp, 2))
    second_slots = [0, 2, 6, 4] if n_dp == 8 else list(range(0, n_dp, 2))

    def rows_of(array, slot):
        return array[slot * shard : (slot + 1) * shard]

    def exchange(outward, inward):
        return along(jnp.where(is_middle, outward, inward), PAIRS)

    def swap_dp(value, bit):
        return lax.ppermute(value, "dp", [(i, i ^ bit) for i in range(n_dp)])

    def both_rows(array):
        return jnp.concatenate([array, swap_dp(array, 1)], axis=0)

    def take(array, held, slots, axis, size=None):
        size = size or block
        at = [held.index(k) for k in slots]
        if at == list(range(at[0], at[0] + len(at))):
            return lax.slice_in_dim(array, at[0] * size, (at[-1] + 1) * size, axis=axis)
        return jnp.concatenate(
            [lax.slice_in_dim(array, i * size, (i + 1) * size, axis=axis) for i in at], axis=axis
        )

    def column_blocks(array):
        def pick(slots):
            return jnp.concatenate(
                [
                    lax.dynamic_slice_in_dim(array, (me_dp ^ k) * block, block, axis=1)
                    for k in slots
                ],
                axis=1,
            )

        theirs = swap_dp(pick([k ^ 1 for k in even_slots]), 1)
        return jnp.concatenate([pick(even_slots), theirs], axis=0)

    half = block // 2

    def half_columns(array):
        def pick(odd):
            cuts = [(k, 0) for k in even_slots] + [(k, half) for k in second_slots]
            return jnp.concatenate(
                [
                    lax.dynamic_slice_in_dim(
                        array, (me_dp ^ k ^ odd) * block + shift, half, axis=1
                    )
                    for k, shift in cuts
                ],
                axis=1,
            )

        joined = jnp.concatenate([pick(0), swap_dp(pick(1), 1)], axis=0)
        return joined

    def half_sums(columns, other, side, stage, gots):
        order = (order_one, order_two)[side]
        held = (even_slots, second_slots)[side]
        base = side * len(even_slots) * half
        cut = lax.slice_in_dim(columns, base, base + len(even_slots) * half, axis=1)
        slots = away_slots(order, stage)
        total = dot_tn(take(cut, held, slots, 1, half), other)
        for earlier, got in enumerate(gots):
            there = [k ^ order[earlier] for k in away_slots(order, earlier)]
            total = total + take(got, there, slots, 0, half).astype(F32)
        return total

    def send_halves(pair_of_halves, stage):
        return [
            swap_dp(part, order[stage])
            for part, order in zip(pair_of_halves, (order_one, order_two))
        ]

    def final_rows(columns, other, gots):
        last = len(order_one)
        if even_slots[-1] == second_slots[0] == 0:
            at = (len(even_slots) - 1) * half
            total = dot_tn(lax.slice_in_dim(columns, at, at + block, axis=1), other)
            parts = [total[:half], total[half:]]
            for side, order in enumerate((order_one, order_two)):
                for stage, got in enumerate(gots[side]):
                    there = [k ^ order[stage] for k in away_slots(order, stage)]
                    parts[side] = parts[side] + take(got, there, [0], 0, half).astype(F32)
        else:
            parts = [half_sums(columns, other, side, last, gots[side]) for side in (0, 1)]
        return jnp.concatenate(parts, axis=0)

    def away_slots(order, stage):
        if stage == len(order):
            return [0]
        return [
            k for k in even_slots if k & order[stage] and not any(k & b for b in order[:stage])
        ]

    def block_sums(blocks, other, axis, order, gots):
        slots = away_slots(order, len(gots))
        picked = take(blocks, even_slots, slots, 1)
        total = dot_tn(picked, other) if axis == 0 else dot_tn(other, picked)
        for stage, got in enumerate(gots):
            held = [k ^ order[stage] for k in away_slots(order, stage)]
            total = total + take(got, held, slots, axis).astype(F32)
        return total

    def pass_on(sums, gots):
        blocks, other, axis, order = sums
        while True:
            go = block_sums(*sums, gots).astype(BF)
            gots.append(swap_dp(go, order[len(gots)]))
            if len(gots) == len(order):
                return go

    inputs = tokens.astype(F32)
    scale_one = lax.rsqrt(jnp.mean(inputs * inputs, axis=-1, keepdims=True) + EPSILON)
    normed = (inputs * scale_one * gain_attn).astype(BF)
    one = along(normed, PAIRS)
    near = along(normed, MIDDLE)
    w_qkv = jnp.concatenate([w_query, w_key, w_value], axis=1)
    qkv_0 = dot(normed, w_qkv).astype(BF)
    near, one = after(near, qkv_0), after(one, qkv_0)
    far = along(one, MIDDLE)
    two = exchange(near, out_cotangent)
    qkv_1 = dot(one, w_qkv).astype(BF)
    cot_near = along(after(out_cotangent, qkv_1), MIDDLE)
    far, two = after(far, qkv_1), after(two, qkv_1)
    three = along(far, OUTWARD)
    cot_1 = two
    slot_2 = jnp.where(is_middle, near, two)
    qkv_2 = dot(slot_2, w_qkv).astype(BF)
    cot_far = along(after(cot_1, slot_2), MIDDLE)
    three = after(three, qkv_2, cot_near)
    slot_3 = jnp.where(is_middle, far, three)
    qkv_3 = dot(slot_3, w_qkv).astype(BF)
    normed_full = jnp.concatenate([normed, one, slot_2, slot_3], axis=0)
    qkv = jnp.concatenate([qkv_0, qkv_1, qkv_2, qkv_3], axis=0)
    mixed = attention(places, bound, qkv)

    third = dot(rows_of(mixed, 3), w_out).astype(BF)
    edge = exchange(out_cotangent, third)
    second = dot(after(rows_of(mixed, 2), third), w_out).astype(BF)
    first = dot(after(rows_of(mixed, 1), third), w_out)
    zeroth = dot(after(rows_of(mixed, 0), third), w_out)
    edge = after(edge, second, first, zeroth)
    across = along(third + edge, MIDDLE)
    edge_two = exchange(cot_near, after(second, edge))
    cot_1 = jnp.where(is_middle, cot_1, edge)
    mixed_both = both_rows(after(mixed, edge))
    normed_blocks = column_blocks(after(normed_full, edge))
    across, edge_two, cot_far = (
        after(across, mixed_both, normed_blocks, cot_1),
        after(edge_two, mixed_both, normed_blocks, cot_1),
        after(cot_far, mixed_both, normed_blocks, cot_1),
    )
    pair = along((first + across.astype(F32)).astype(BF), PAIRS)
    middle = along(second + edge_two, MIDDLE)
    cot_2 = jnp.where(is_middle, cot_near, edge_two)
    cot_three = along(after(cot_far, cot_2), OUTWARD)
    back_012 = dot_nt(jnp.concatenate([out_cotangent, cot_1, cot_2], axis=0), w_down).astype(BF)
    pair, middle = after(pair, back_012), after(middle, back_012)
    resid = inputs + (zeroth + pair.astype(F32) + middle.astype(F32))

    scale_two = lax.rsqrt(jnp.mean(resid * resid, axis=-1, keepdims=True) + EPSILON)
    normed_two = (resid * scale_two * gain_mlp).astype(BF)

    units = w_gate.shape[1]
    wide = -(-units // LANES) * LANES

    def feed(slot_rows, back):
        gate = dot(slot_rows, w_gate)
        upward = dot(slot_rows, w_up)
        sig = jax.nn.sigmoid(gate)
        active = gate * sig
        back = back.astype(F32)
        hid = (active * upward).astype(BF)
        d_g = (back * upward * sig * (1.0 + gate * (1.0 - sig))).astype(BF)
        d_u = (back * active).astype(BF)
        d_both = jnp.concatenate(
            [jnp.pad(d, ((0, 0), (0, wide - units))) for d in (d_g, d_u)], axis=1
        )
        return hid, lax.optimization_barrier(d_both)

    def unfeed(fed):
        d_both = fed[1]
        return dot_nt(d_both[:, :units], w_gate) + dot_nt(d_both[:, wide : wide + units], w_up)

    one = along(normed_two, PAIRS)
    near = along(normed_two, MIDDLE)
    fed_0 = feed(normed_two, rows_of(back_012, 0))
    part_0 = unfeed(fed_0)
    near, one = after(near, part_0), after(one, part_0)
    two = along(near, OUTWARD)
    far = along(one, MIDDLE)
    fed_1 = feed(one, rows_of(back_012, 1))
    part_1 = unfeed(fed_1)
    out_1 = dot(fed_1[0], w_down)
    cot_3 = jnp.where(is_middle, cot_far, after(cot_three, one))
    back_3 = dot_nt(cot_3, w_down).astype(BF)
    far, two = after(far, part_1, out_1, back_3), after(two, part_1, out_1, back_3)
    three = exchange(far, out_1.astype(BF))
    cot_full = jnp.concatenate([out_cotangent, cot_1, cot_2, after(cot_3, two)], axis=0)
    cot_columns = half_columns(cot_full)
    slot_2 = jnp.where(is_middle, near, two)
    fed_2 = feed(slot_2, rows_of(back_012, 2))
    part_2 = unfeed(fed_2).astype(BF)
    three = after(three, part_2, cot_columns)
    out_in = three
    slot_3 = jnp.where(is_middle, far, three)
    fed_3 = feed(slot_3, back_3)
    third = unfeed(fed_3).astype(BF)

    edge = along(third, INWARD)
    hidden_s, d_feed_s = zip(fed_0, fed_1, fed_2, fed_3)
    hidden_both = both_rows(after(jnp.concatenate(hidden_s, axis=0), third))
    second_full = jnp.concatenate([normed_two, one, slot_2, slot_3], axis=0)
    down_pay = [half_sums(cot_columns, hidden_both, side, 0, []).astype(BF) for side in (0, 1)]
    down_got = send_halves(down_pay, 0)
    edge = after(edge, *down_pay)
    across = along(third + edge, MIDDLE)
    edge_two = along(after(part_2, edge), INWARD)
    second_columns = half_columns(after(second_full, edge))
    d_feed = jnp.concatenate(d_feed_s, axis=0)
    feed_both = both_rows(after(d_feed, edge))
    feed_pay = [half_sums(second_columns, feed_both, side, 0, []).astype(BF) for side in (0, 1)]
    across, edge_two = after(across, *feed_pay), after(edge_two, *feed_pay)
    pair = along((part_1 + across.astype(F32)).astype(BF), PAIRS)
    middle = along(part_2 + edge_two, MIDDLE)
    down_got = [after(g, *feed_pay) for g in down_got]
    feed_got = send_halves([after(p, *down_got) for p in feed_pay], 0)
    out_3 = dot(after(fed_3[0], across), w_down).astype(BF)
    pair = after(pair, out_3)
    d_normed_two = part_0 + pair.astype(F32) + middle.astype(F32)
    weighted_two = d_normed_two * gain_mlp
    d_resid = (
        out_cotangent.astype(F32)
        + scale_two * weighted_two
        - resid * scale_two**3 * jnp.mean(weighted_two * resid, axis=-1, keepdims=True)
    )
    d_attn = d_resid.astype(BF)

    one = along(d_attn, PAIRS)
    near = along(d_attn, MIDDLE)
    gain_two_part = jnp.sum(d_normed_two * resid * scale_two, axis=0)
    out_2 = dot(after(fed_2[0], d_attn), w_down).astype(BF)
    out_0 = dot(after(fed_0[0], d_attn), w_down)
    early = (gain_two_part, out_0, out_2)
    near, one = after(near, *early), after(one, *early)
    far = along(one, MIDDLE)
    two = exchange(near, out_3)
    d_mixed_0 = dot_nt(after(d_attn, one), w_out).astype(BF)
    d_mixed_1 = dot_nt(after(one, d_mixed_0), w_out).astype(BF)
    far, two = after(far, d_mixed_1), after(two, d_mixed_1)
    three = exchange(far, out_2)
    slot_2 = jnp.where(is_middle, near, two)
    d_mixed_2 = dot_nt(slot_2, w_out).astype(BF)
    out_across = along(out_3 + after(two, d_mixed_2), MIDDLE)
    before = attention_back(
        places, bound, qkv, jnp.concatenate([d_mixed_0, d_mixed_1, d_mixed_2], axis=0), 0, None
    )
    feed_got = [after(g, d_mixed_1) for g in feed_got]
    feed_gots = [[g] for g in feed_got]
    down_gots = [[g] for g in down_got]
    for stage in range(1, len(order_one)):
        rest = [
            jnp.concatenate(
                [
                    half_sums(second_columns, feed_both, side, stage, feed_gots[side]),
                    half_sums(cot_columns, hidden_both, side, stage, down_gots[side]),
                ],
                axis=1,
            ).astype(BF)
            for side in (0, 1)
        ]
        for side, got in enumerate(send_halves(rest, stage)):
            got = after(got, before[0])
            feed_gots[side].append(got[:, : d_feed.shape[1]])
            down_gots[side].append(got[:, d_feed.shape[1] :])
    rest_got = got
    three = after(three, before[0])
    slot_3 = jnp.where(is_middle, far, three)
    d_mixed_3 = dot_nt(slot_3, w_out).astype(BF)
    d_qkv = attention_back(places, bound, qkv, d_mixed_3, 3 * shard, before)

    third = dot_nt(rows_of(d_qkv, 3), w_qkv).astype(BF)
    edge = along(third, INWARD)
    qkv_both = both_rows(after(d_qkv, third))
    second = dot_nt(after(rows_of(d_qkv, 2), third), w_qkv).astype(BF)
    first = dot_nt(after(rows_of(d_qkv, 1), third), w_qkv)
    zeroth = dot_nt(after(rows_of(d_qkv, 0), third), w_qkv)
    out_middle = along(after(out_2 + three, second), MIDDLE)
    out_sum = (out_1 + after(out_across, second).astype(F32)).astype(BF)
    d_normed_part = jnp.concatenate([zeroth, first, second.astype(F32), third.astype(F32)], axis=0)
    gain_one_part = jnp.sum(d_normed_part * normed_full.astype(F32), axis=0)
    gains = jnp.stack([gain_one_part / gain_attn, gain_two_part])
    gains = gains + swap_dp(gains, bits[0])
    gains_got = swap_dp(gains, bits[1])
    of_qkv = (normed_blocks, after(qkv_both, gains), 0, order_one)
    qkv_go = block_sums(*of_qkv, []).astype(BF)
    qkv_got = swap_dp(qkv_go, order_one[0])
    edge = after(edge, out_sum, gains, rest_got)
    across = along(third + edge, MIDDLE)
    edge_two = exchange(out_sum, after(second, edge))
    gains = gains + after(gains_got, edge)
    for bit in bits[2:]:
        gains = gains + swap_dp(gains, bit)
    attn_full = jnp.concatenate([d_attn, one, slot_2, slot_3], axis=0)
    attn_blocks = column_blocks(after(attn_full, third))
    of_out = (attn_blocks, mixed_both, 1, order_two)
    out_go = block_sums(*of_out, []).astype(BF)
    out_got = swap_dp(out_go, order_two[0])
    across, edge_two = after(across, gains, out_go), after(edge_two, gains, out_go)
    gains_there = gains
    gains = gains.astype(BF)
    pair = along(
        jnp.concatenate([(first + across.astype(F32)).astype(BF), gains], axis=0), PAIRS
    )
    middle = along(second + edge_two, MIDDLE)
    qkv_gots = [after(qkv_got, across)]
    qkv_mid = pass_on(of_qkv, qkv_gots)
    out_gots = [after(out_got, across)]
    out_back = pass_on(of_out, out_gots)
    gains = gains.astype(F32) + pair[shard:].astype(F32)
    gains = gains + along(gains, [(i, i ^ 2) for i in range(4)])
    pair = pair[:shard]
    grad_down = final_rows(after(cot_columns, qkv_mid), hidden_both, down_gots).T
    feed_late = [[after(g, gains_there) for g in side] for side in feed_gots]
    grad_feed = final_rows(after(second_columns, gains_there), feed_both, feed_late)
    grad_qkv = block_sums(*of_qkv, qkv_gots)
    grad_out = block_sums(*of_out, out_gots)
    out_rest = jnp.where(
        is_middle, out_in.astype(F32) + after(out_middle, across).astype(F32), edge_two.astype(F32)
    )
    outputs = (resid + (out_0 + out_rest)).astype(BF)
    d_normed = zeroth + pair.astype(F32) + middle.astype(F32)
    weighted_one = d_normed * gain_attn
    grad_tokens = (
        d_resid
        + scale_one * weighted_one
        - inputs * scale_one**3 * jnp.mean(weighted_one * inputs, axis=-1, keepdims=True)
    )
    return (
        outputs,
        grad_tokens,
        grad_qkv[:, :n_q],
        grad_qkv[:, n_q : 2 * n_q],
        grad_qkv[:, 2 * n_q :],
        grad_out,
        grad_feed[:, :units],
        grad_feed[:, wide : wide + units],
        grad_down,
        gains[0],
        gains[1],
    )


def solution(mesh):
    return jax.shard_map(
        on_device,
        mesh=mesh,
        in_specs=(
            P(("dp", "mp"), None),
            P("dp"),
            P(None, "mp"),
            P(None, "mp"),
            P(None, "mp"),
            P("mp", None),
            P(None, "mp"),
            P(None, "mp"),
            P("mp", None),
            P(),
            P(),
            P(("dp", "mp"), None),
        ),
        out_specs=(
            P(("dp", "mp"), None),
            P(("dp", "mp"), None),
            P("dp", "mp"),
            P("dp", "mp"),
            P("dp", "mp"),
            P("mp", "dp"),
            P("dp", "mp"),
            P("dp", "mp"),
            P("mp", "dp"),
            P(),
            P(),
        ),
        check_vma=False,
    )
```

```python
import functools

import jax
import jax.numpy as jnp
from jax import lax
from jax.experimental import pallas as pl
from jax.experimental.pallas import tpu as pltpu
from jax.sharding import PartitionSpec as P

FK = 16
DV = 128
BF = jnp.bfloat16
F32 = jnp.float32
EPSILON = 1e-06
BLOCK = 128
UNSEEN = 1 << 24
LANES = 128

PAIRS = [(0, 1), (1, 0), (2, 3), (3, 2)]
MIDDLE = [(1, 2), (2, 1)]
OUTWARD = [(2, 3), (1, 0)]
INWARD = [(3, 2), (0, 1)]


def dot(left, right):
    return jnp.dot(left, right, preferred_element_type=F32)


def dot_nt(left, right):
    return lax.dot_general(left, right, (((1,), (1,)), ((), ())), preferred_element_type=F32)


def dot_tn(left, right):
    return lax.dot_general(left, right, (((0,), (0,)), ((), ())), preferred_element_type=F32)


def head_lanes(array, head):
    lane = lax.broadcasted_iota(jnp.int32, array.shape, 1) // FK
    return jnp.where(lane == head, array.astype(F32), 0.0).astype(BF)


def weights_of(query, key, seen):
    inner = dot_nt(query, key)
    weight = jnp.where(seen, 1.0 + inner * (0.25 + inner * (1.0 / 32.0)), 0.0)
    return inner, weight, 1.0 / jnp.sum(weight, axis=-1, keepdims=True)


def attention_kernel(heads, place_ref, bound_ref, qkv_ref, mixed_ref):
    n_q = heads * FK
    key = qkv_ref[:, n_q : 2 * n_q]
    queries = [head_lanes(qkv_ref[:, :n_q], h) for h in range(heads)]
    bound = bound_ref[...]
    for first in range(0, qkv_ref.shape[0], BLOCK):
        seen = bound <= place_ref[first : first + BLOCK]
        for h in range(heads):
            _, weight, scale = weights_of(queries[h][first : first + BLOCK], key, seen)
            value = qkv_ref[:, 2 * n_q + h * DV : 2 * n_q + (h + 1) * DV]
            mixed_ref[first : first + BLOCK, h * DV : (h + 1) * DV] = dot(
                (weight * scale).astype(BF), value
            ).astype(BF)


def cost(flops):
    return pl.CostEstimate(flops=flops, bytes_accessed=2**21, transcendentals=0)


def attention(place, bound, qkv):
    heads = (qkv.shape[1] // (2 * FK + DV))
    return pl.pallas_call(
        functools.partial(attention_kernel, heads),
        out_shape=jax.ShapeDtypeStruct((qkv.shape[0], heads * DV), BF),
        compiler_params=pltpu.CompilerParams(vmem_limit_bytes=32 * 2**20),
        cost_estimate=cost(qkv.shape[0] * qkv.shape[0] * heads * 2 * (2 * FK + DV) * 16),
        name="attention",
    )(place, bound, qkv)


def attention_back_kernel(heads, start, last, *refs):
    if last:
        place_ref, bound_ref, qkv_ref, d_mixed_ref, query_ref, total_ref, out_ref = refs
    else:
        place_ref, bound_ref, qkv_ref, d_mixed_ref, query_ref, total_ref = refs
    n_q = heads * FK
    key = qkv_ref[:, n_q : 2 * n_q]
    keys = [head_lanes(key, h) for h in range(heads)]
    bound = bound_ref[...]
    rows = d_mixed_ref.shape[0]
    d_key = 0.0
    d_values = [0.0] * heads
    for first in range(0, rows, BLOCK):
        here = slice(start + first, start + first + BLOCK)
        seen = bound <= place_ref[here]
        d_query = 0.0
        for h in range(heads):
            query = head_lanes(qkv_ref[here, :n_q], h)
            inner, weight, scale = weights_of(query, key, seen)
            share = weight * scale
            value = qkv_ref[:, 2 * n_q + h * DV : 2 * n_q + (h + 1) * DV]
            d_out = d_mixed_ref[first : first + BLOCK, h * DV : (h + 1) * DV]
            d_share = dot_nt(d_out, value)
            row = jnp.sum(d_share * share, axis=-1, keepdims=True)
            d_inner = jnp.where(
                seen, (d_share - row) * scale * (0.25 + inner * (1.0 / 16.0)), 0.0
            ).astype(BF)
            d_query = d_query + dot(d_inner, keys[h])
            d_key = d_key + dot_tn(d_inner, query)
            d_values[h] = d_values[h] + dot_tn(share.astype(BF), d_out)
        if last:
            out_ref[here, :n_q] = d_query.astype(BF)
        else:
            query_ref[first : first + BLOCK] = d_query.astype(BF)
    if last:
        out_ref[:start, :n_q] = query_ref[...]
        out_ref[:, n_q : 2 * n_q] = (d_key + total_ref[:, heads * DV :]).astype(BF)
        for h in range(heads):
            out_ref[:, 2 * n_q + h * DV : 2 * n_q + (h + 1) * DV] = (
                d_values[h] + total_ref[:, h * DV : (h + 1) * DV]
            ).astype(BF)
    else:
        total_ref[:, heads * DV :] = d_key
        for h in range(heads):
            total_ref[:, h * DV : (h + 1) * DV] = d_values[h]


def attention_back(place, bound, qkv, d_mixed, start, before):
    heads = (qkv.shape[1] // (2 * FK + DV))
    n_q = heads * FK
    rows = d_mixed.shape[0]
    last = before is not None
    if last:
        shape = jax.ShapeDtypeStruct(qkv.shape, BF)
    else:
        shape = (
            jax.ShapeDtypeStruct((rows, n_q), BF),
            jax.ShapeDtypeStruct((qkv.shape[0], n_q + heads * DV), F32),
        )
    return pl.pallas_call(
        functools.partial(attention_back_kernel, heads, start, last),
        out_shape=shape,
        compiler_params=pltpu.CompilerParams(vmem_limit_bytes=40 * 2**20),
        cost_estimate=cost(rows * qkv.shape[0] * heads * 2 * (6 * FK + 2 * DV)),
        name="attention_back",
    )(place, bound, qkv, d_mixed, *(before or ()))


def after(value, *others):
    return lax.optimization_barrier((value, *others))[0]


def along(value, pairs):
    return lax.ppermute(value, "mp", pairs)


def on_device(
    tokens,
    lengths,
    w_query,
    w_key,
    w_value,
    w_out,
    w_gate,
    w_up,
    w_down,
    gain_attn,
    gain_mlp,
    out_cotangent,
):
    shard = tokens.shape[0]
    width = tokens.shape[1]
    heads = w_query.shape[1] // FK
    n_q = w_query.shape[1]
    n_dp = lax.axis_size("dp")
    block = width // n_dp
    bits = [1 << b for b in range(n_dp.bit_length() - 1)]
    me_mp = lax.axis_index("mp")
    me_dp = lax.axis_index("dp")
    is_middle = (me_mp == 1) | (me_mp == 2)
    chunk_ids = [
        me_mp,
        me_mp ^ 1,
        jnp.where(is_middle, me_mp ^ 3, me_mp ^ 2),
        jnp.where(is_middle, me_mp ^ 2, me_mp ^ 3),
    ]
    places = jnp.concatenate([c * shard + jnp.arange(shard, dtype=jnp.int32) for c in chunk_ids])
    bound = jnp.where(places < lengths[0], places, UNSEEN)[None, :]
    places = places[:, None]

    order_one = bits[1:]
    order_two = order_one[::-1]
    even_slots = [2, 6, 4, 0] if n_dp == 8 else list(range(0, n_dp, 2))
    second_slots = [0, 2, 6, 4] if n_dp == 8 else list(range(0, n_dp, 2))

    def rows_of(array, slot):
        return array[slot * shard : (slot + 1) * shard]

    def exchange(outward, inward):
        return along(jnp.where(is_middle, outward, inward), PAIRS)

    def swap_dp(value, bit):
        return lax.ppermute(value, "dp", [(i, i ^ bit) for i in range(n_dp)])

    def both_rows(array):
        return jnp.concatenate([array, swap_dp(array, 1)], axis=0)

    def take(array, held, slots, axis, size=None):
        size = size or block
        at = [held.index(k) for k in slots]
        if at == list(range(at[0], at[0] + len(at))):
            return lax.slice_in_dim(array, at[0] * size, (at[-1] + 1) * size, axis=axis)
        return jnp.concatenate(
            [lax.slice_in_dim(array, i * size, (i + 1) * size, axis=axis) for i in at], axis=axis
        )

    def column_blocks(array):
        def pick(slots):
            return jnp.concatenate(
                [
                    lax.dynamic_slice_in_dim(array, (me_dp ^ k) * block, block, axis=1)
                    for k in slots
                ],
                axis=1,
            )

        theirs = swap_dp(pick([k ^ 1 for k in even_slots]), 1)
        return jnp.concatenate([pick(even_slots), theirs], axis=0)

    half = block // 2

    def half_picks(array):
        def pick(odd):
            cuts = [(k, 0) for k in even_slots] + [(k, half) for k in second_slots]
            return jnp.concatenate(
                [
                    lax.dynamic_slice_in_dim(
                        array, (me_dp ^ k ^ odd) * block + shift, half, axis=1
                    )
                    for k, shift in cuts
                ],
                axis=1,
            )

        return pick(0), swap_dp(pick(1), 1)

    def half_columns(array):
        return jnp.concatenate(half_picks(array), axis=0)

    def half_sums(columns, other, side, stage, gots):
        order = (order_one, order_two)[side]
        held = (even_slots, second_slots)[side]
        base = side * len(even_slots) * half
        cut = lax.slice_in_dim(columns, base, base + len(even_slots) * half, axis=1)
        slots = away_slots(order, stage)
        total = dot_tn(take(cut, held, slots, 1, half), other)
        for earlier, got in enumerate(gots):
            there = [k ^ order[earlier] for k in away_slots(order, earlier)]
            total = total + take(got, there, slots, 0, half).astype(F32)
        return total

    def send_halves(pair_of_halves, stage):
        return [
            swap_dp(part, order[stage])
            for part, order in zip(pair_of_halves, (order_one, order_two))
        ]

    def final_product(columns, other):
        at = (len(even_slots) - 1) * half
        if even_slots[-1] == second_slots[0] == 0:
            total = dot_tn(lax.slice_in_dim(columns, at, at + block, axis=1), other)
            return total[:half], total[half:]
        return [half_sums(columns, other, side, len(order_one), []) for side in (0, 1)]

    def final_rows(parts, gots):
        parts = list(parts)
        for side, order in enumerate((order_one, order_two)):
            for stage, got in enumerate(gots[side]):
                there = [k ^ order[stage] for k in away_slots(order, stage)]
                parts[side] = parts[side] + take(got, there, [0], 0, half).astype(F32)
        return jnp.concatenate(parts, axis=0)

    def away_slots(order, stage):
        if stage == len(order):
            return [0]
        return [
            k for k in even_slots if k & order[stage] and not any(k & b for b in order[:stage])
        ]

    def block_sums(blocks, other, axis, order, gots, total=None):
        slots = away_slots(order, len(gots))
        picked = take(blocks, even_slots, slots, 1)
        if total is None:
            total = dot_tn(picked, other) if axis == 0 else dot_tn(other, picked)
        for stage, got in enumerate(gots):
            held = [k ^ order[stage] for k in away_slots(order, stage)]
            total = total + take(got, held, slots, axis).astype(F32)
        return total

    def pass_on(sums, gots):
        blocks, other, axis, order = sums
        while True:
            go = block_sums(*sums, gots).astype(BF)
            gots.append(swap_dp(go, order[len(gots)]))
            if len(gots) == len(order):
                return go

    inputs = tokens.astype(F32)
    scale_one = lax.rsqrt(jnp.mean(inputs * inputs, axis=-1, keepdims=True) + EPSILON)
    normed = (inputs * scale_one * gain_attn).astype(BF)
    one = along(normed, PAIRS)
    near = along(normed, MIDDLE)
    w_qkv = jnp.concatenate([w_query, w_key, w_value], axis=1)
    qkv_0 = dot(normed, w_qkv).astype(BF)
    near, one = after(near, qkv_0), after(one, qkv_0)
    far = along(one, MIDDLE)
    two = exchange(near, out_cotangent)
    qkv_1 = dot(one, w_qkv).astype(BF)
    cot_near = along(after(out_cotangent, qkv_1), MIDDLE)
    far, two = after(far, qkv_1), after(two, qkv_1)
    three = along(far, OUTWARD)
    cot_1 = two
    slot_2 = jnp.where(is_middle, near, two)
    qkv_2 = dot(slot_2, w_qkv).astype(BF)
    cot_far = along(after(cot_1, slot_2), MIDDLE)
    three = after(three, qkv_2, cot_near)
    slot_3 = jnp.where(is_middle, far, three)
    qkv_3 = dot(slot_3, w_qkv).astype(BF)
    normed_full = jnp.concatenate([normed, one, slot_2, slot_3], axis=0)
    qkv = jnp.concatenate([qkv_0, qkv_1, qkv_2, qkv_3], axis=0)
    mixed = attention(places, bound, qkv)

    third = dot(rows_of(mixed, 3), w_out).astype(BF)
    edge = exchange(out_cotangent, third)
    second = dot(after(rows_of(mixed, 2), third), w_out).astype(BF)
    first = dot(after(rows_of(mixed, 1), third), w_out)
    zeroth = dot(after(rows_of(mixed, 0), third), w_out)
    edge = after(edge, second, first, zeroth)
    across = along(third + edge, MIDDLE)
    edge_two = exchange(cot_near, after(second, edge))
    cot_1 = jnp.where(is_middle, cot_1, edge)
    mixed_both = both_rows(after(mixed, edge))
    normed_blocks = column_blocks(after(normed_full, edge))
    across, edge_two, cot_far = (
        after(across, mixed_both, normed_blocks, cot_1),
        after(edge_two, mixed_both, normed_blocks, cot_1),
        after(cot_far, mixed_both, normed_blocks, cot_1),
    )
    pair = along((first + across.astype(F32)).astype(BF), PAIRS)
    middle = along(second + edge_two, MIDDLE)
    cot_2 = jnp.where(is_middle, cot_near, edge_two)
    cot_three = along(after(cot_far, cot_2), OUTWARD)
    cot_012 = jnp.concatenate([out_cotangent, cot_1, cot_2], axis=0)
    back_012 = dot_nt(cot_012, w_down).astype(BF)
    cot_early = half_picks(cot_012)
    pair, middle = after(pair, back_012), after(middle, back_012)
    resid = inputs + (zeroth + pair.astype(F32) + middle.astype(F32))

    scale_two = lax.rsqrt(jnp.mean(resid * resid, axis=-1, keepdims=True) + EPSILON)
    normed_two = (resid * scale_two * gain_mlp).astype(BF)

    units = w_gate.shape[1]
    wide = -(-units // LANES) * LANES

    def feed(slot_rows, back):
        gate = dot(slot_rows, w_gate)
        upward = dot(slot_rows, w_up)
        sig = jax.nn.sigmoid(gate)
        active = gate * sig
        back = back.astype(F32)
        hid = (active * upward).astype(BF)
        d_g = (back * upward * sig * (1.0 + gate * (1.0 - sig))).astype(BF)
        d_u = (back * active).astype(BF)
        d_both = jnp.concatenate(
            [jnp.pad(d, ((0, 0), (0, wide - units))) for d in (d_g, d_u)], axis=1
        )
        return hid, lax.optimization_barrier(d_both)

    def unfeed(fed):
        d_both = fed[1]
        return dot_nt(d_both[:, :units], w_gate) + dot_nt(d_both[:, wide : wide + units], w_up)

    one = along(normed_two, PAIRS)
    near = along(normed_two, MIDDLE)
    fed_0 = feed(normed_two, rows_of(back_012, 0))
    part_0 = unfeed(fed_0)
    near, one = after(near, part_0), after(one, part_0)
    two = along(near, OUTWARD)
    far = along(one, MIDDLE)
    fed_1 = feed(one, rows_of(back_012, 1))
    part_1 = unfeed(fed_1)
    out_1 = dot(fed_1[0], w_down)
    cot_3 = jnp.where(is_middle, cot_far, after(cot_three, one))
    back_3 = dot_nt(cot_3, w_down).astype(BF)
    far, two = after(far, part_1, out_1, back_3), after(two, part_1, out_1, back_3)
    three = exchange(far, out_1.astype(BF))
    cot_full = jnp.concatenate([out_cotangent, cot_1, cot_2, after(cot_3, two)], axis=0)
    slot_2 = jnp.where(is_middle, near, two)
    fed_2 = feed(slot_2, rows_of(back_012, 2))
    part_2 = unfeed(fed_2).astype(BF)
    three = after(three, part_2)
    out_in = three
    slot_3 = jnp.where(is_middle, far, three)
    fed_3 = feed(slot_3, back_3)
    third = unfeed(fed_3).astype(BF)

    edge = along(third, INWARD)
    hidden_s, d_feed_s = zip(fed_0, fed_1, fed_2, fed_3)
    hidden_both = both_rows(after(jnp.concatenate(hidden_s, axis=0), third))
    second_full = jnp.concatenate([normed_two, one, slot_2, slot_3], axis=0)
    cot_late = half_picks(after(cot_3, third))
    cot_columns = jnp.concatenate([cot_early[0], cot_late[0], cot_early[1], cot_late[1]], axis=0)
    down_pay = [half_sums(cot_columns, hidden_both, side, 0, []).astype(BF) for side in (0, 1)]
    down_got = send_halves(down_pay, 0)
    edge = after(edge, *down_pay)
    across = along(third + edge, MIDDLE)
    edge_two = along(after(part_2, edge), INWARD)
    second_columns = half_columns(after(second_full, edge))
    d_feed = jnp.concatenate(d_feed_s, axis=0)
    feed_both = both_rows(after(d_feed, edge))
    feed_pay = [half_sums(second_columns, feed_both, side, 0, []).astype(BF) for side in (0, 1)]
    across, edge_two = after(across, *feed_pay), after(edge_two, *feed_pay)
    pair = along((part_1 + across.astype(F32)).astype(BF), PAIRS)
    middle = along(part_2 + edge_two, MIDDLE)
    down_got = [after(g, *feed_pay) for g in down_got]
    feed_got = send_halves([after(p, *down_got) for p in feed_pay], 0)
    out_3 = dot(after(fed_3[0], across), w_down).astype(BF)
    pair = after(pair, out_3)
    d_normed_two = part_0 + pair.astype(F32) + middle.astype(F32)
    weighted_two = d_normed_two * gain_mlp
    d_resid = (
        out_cotangent.astype(F32)
        + scale_two * weighted_two
        - resid * scale_two**3 * jnp.mean(weighted_two * resid, axis=-1, keepdims=True)
    )
    d_attn = d_resid.astype(BF)

    one = along(d_attn, PAIRS)
    near = along(d_attn, MIDDLE)
    gain_two_part = jnp.sum(d_normed_two * resid * scale_two, axis=0)
    out_2 = dot(after(fed_2[0], d_attn), w_down).astype(BF)
    out_0 = dot(after(fed_0[0], d_attn), w_down)
    feed_stays = final_product(after(second_columns, d_attn), feed_both)
    down_stays = final_product(after(cot_columns, d_attn), hidden_both)
    early = (gain_two_part, out_0, out_2)
    near, one = after(near, *early), after(one, *early)
    far = along(one, MIDDLE)
    two = exchange(near, out_3)
    d_mixed_0 = dot_nt(after(d_attn, one), w_out).astype(BF)
    d_mixed_1 = dot_nt(after(one, d_mixed_0), w_out).astype(BF)
    far, two = after(far, d_mixed_1), after(two, d_mixed_1)
    three = exchange(far, out_2)
    slot_2 = jnp.where(is_middle, near, two)
    d_mixed_2 = dot_nt(slot_2, w_out).astype(BF)
    out_across = along(out_3 + after(two, d_mixed_2), MIDDLE)
    before = attention_back(
        places, bound, qkv, jnp.concatenate([d_mixed_0, d_mixed_1, d_mixed_2], axis=0), 0, None
    )
    feed_got = [after(g, d_mixed_1) for g in feed_got]
    feed_gots = [[g] for g in feed_got]
    down_gots = [[g] for g in down_got]
    rests = []
    for stage in range(1, len(order_one)):
        rest = [
            jnp.concatenate(
                [
                    half_sums(second_columns, feed_both, side, stage, feed_gots[side]),
                    half_sums(cot_columns, hidden_both, side, stage, down_gots[side]),
                ],
                axis=1,
            ).astype(BF)
            for side in (0, 1)
        ]
        rest_got = [after(got, before[0]) for got in send_halves(rest, stage)]
        rests.append(rest_got)
        for side, got in enumerate(rest_got):
            feed_gots[side].append(got[:, : d_feed.shape[1]])
            down_gots[side].append(got[:, d_feed.shape[1] :])
    three = after(three, before[0])
    slot_3 = jnp.where(is_middle, far, three)
    d_mixed_3 = dot_nt(slot_3, w_out).astype(BF)
    d_qkv = attention_back(places, bound, qkv, d_mixed_3, 3 * shard, before)

    third = dot_nt(rows_of(d_qkv, 3), w_qkv).astype(BF)
    edge = along(third, INWARD)
    qkv_both = both_rows(after(d_qkv, third))
    second = dot_nt(after(rows_of(d_qkv, 2), third), w_qkv).astype(BF)
    first = dot_nt(after(rows_of(d_qkv, 1), third), w_qkv)
    zeroth = dot_nt(after(rows_of(d_qkv, 0), third), w_qkv)
    out_middle = along(after(out_2 + three, second), MIDDLE)
    out_sum = (out_1 + after(out_across, second).astype(F32)).astype(BF)
    d_normed_part = jnp.concatenate([zeroth, first, second.astype(F32), third.astype(F32)], axis=0)
    gain_one_part = jnp.sum(d_normed_part * normed_full.astype(F32), axis=0)
    gains = jnp.stack([gain_one_part / gain_attn, gain_two_part])
    gains = gains + swap_dp(gains, bits[0])
    gains_got = swap_dp(gains, bits[1])
    of_qkv = (normed_blocks, after(qkv_both, gains), 0, order_one)
    qkv_go = block_sums(*of_qkv, []).astype(BF)
    qkv_got = swap_dp(qkv_go, order_one[0])
    edge = after(edge, out_sum, gains, *rest_got)
    across = along(third + edge, MIDDLE)
    edge_two = exchange(out_sum, after(second, edge))
    gains = gains + after(gains_got, edge)
    for bit in bits[2:]:
        gains = gains + swap_dp(gains, bit)
    attn_full = jnp.concatenate([d_attn, one, slot_2, slot_3], axis=0)
    attn_blocks = column_blocks(after(attn_full, third))
    of_out = (attn_blocks, mixed_both, 1, order_two)
    out_go = block_sums(*of_out, []).astype(BF)
    out_got = swap_dp(out_go, order_two[0])
    across, edge_two = after(across, gains, out_go), after(edge_two, gains, out_go)
    gains_there = gains
    gains = gains.astype(BF)
    pair = along(
        jnp.concatenate([(first + across.astype(F32)).astype(BF), gains], axis=0), PAIRS
    )
    middle = along(second + edge_two, MIDDLE)
    qkv_gots = [after(qkv_got, across)]
    qkv_mid = pass_on(of_qkv, qkv_gots)
    out_gots = [after(out_got, across)]
    out_back = pass_on(of_out, out_gots)
    gains = gains.astype(F32) + pair[shard:].astype(F32)
    gains = gains + along(gains, [(i, i ^ 2) for i in range(4)])
    pair = pair[:shard]
    down_late = [
        [after(down_gots[side][0], qkv_mid)]
        + [after(r[side], qkv_mid)[:, d_feed.shape[1] :] for r in rests]
        for side in (0, 1)
    ]
    grad_down = final_rows(down_stays, down_late).T
    feed_late = [
        [after(feed_gots[side][0], gains_there)]
        + [after(r[side], gains_there)[:, : d_feed.shape[1]] for r in rests]
        for side in (0, 1)
    ]
    grad_feed = final_rows(feed_stays, feed_late)
    qkv_stays = dot_tn(take(after(of_qkv[0], qkv_mid), even_slots, [0], 1), of_qkv[1])
    out_stays = dot_tn(mixed_both, take(after(attn_blocks, qkv_mid), even_slots, [0], 1))
    grad_qkv = block_sums(*of_qkv, qkv_gots, qkv_stays)
    grad_out = block_sums(*of_out, out_gots, out_stays)
    out_rest = jnp.where(
        is_middle, out_in.astype(F32) + after(out_middle, across).astype(F32), edge_two.astype(F32)
    )
    outputs = (resid + (out_0 + out_rest)).astype(BF)
    d_normed = zeroth + pair.astype(F32) + middle.astype(F32)
    weighted_one = d_normed * gain_attn
    grad_tokens = (
        d_resid
        + scale_one * weighted_one
        - inputs * scale_one**3 * jnp.mean(weighted_one * inputs, axis=-1, keepdims=True)
    )
    return (
        outputs,
        grad_tokens,
        grad_qkv[:, :n_q],
        grad_qkv[:, n_q : 2 * n_q],
        grad_qkv[:, 2 * n_q :],
        grad_out,
        grad_feed[:, :units],
        grad_feed[:, wide : wide + units],
        grad_down,
        gains[0],
        gains[1],
    )


def solution(mesh):
    return jax.shard_map(
        on_device,
        mesh=mesh,
        in_specs=(
            P(("dp", "mp"), None),
            P("dp"),
            P(None, "mp"),
            P(None, "mp"),
            P(None, "mp"),
            P("mp", None),
            P(None, "mp"),
            P(None, "mp"),
            P("mp", None),
            P(),
            P(),
            P(("dp", "mp"), None),
        ),
        out_specs=(
            P(("dp", "mp"), None),
            P(("dp", "mp"), None),
            P("dp", "mp"),
            P("dp", "mp"),
            P("dp", "mp"),
            P("mp", "dp"),
            P("dp", "mp"),
            P("dp", "mp"),
            P("mp", "dp"),
            P(),
            P(),
        ),
        check_vma=False,
    )
```

```python
import functools

import jax
import jax.numpy as jnp
from jax import lax
from jax.experimental import pallas as pl
from jax.experimental.pallas import tpu as pltpu
from jax.sharding import PartitionSpec as P

FK = 16
DV = 128
BF = jnp.bfloat16
F32 = jnp.float32
EPSILON = 1e-06
BLOCK = 128
UNSEEN = 1 << 24
LANES = 128

PAIRS = [(0, 1), (1, 0), (2, 3), (3, 2)]
MIDDLE = [(1, 2), (2, 1)]
OUTWARD = [(2, 3), (1, 0)]
INWARD = [(3, 2), (0, 1)]


def dot(left, right):
    return jnp.dot(left, right, preferred_element_type=F32)


def dot_nt(left, right):
    return lax.dot_general(left, right, (((1,), (1,)), ((), ())), preferred_element_type=F32)


def dot_tn(left, right):
    return lax.dot_general(left, right, (((0,), (0,)), ((), ())), preferred_element_type=F32)


def head_lanes(array, head):
    lane = lax.broadcasted_iota(jnp.int32, array.shape, 1) // FK
    return jnp.where(lane == head, array.astype(F32), 0.0).astype(BF)


def weights_of(query, key, seen):
    inner = dot_nt(query, key)
    weight = jnp.where(seen, 1.0 + inner * (0.25 + inner * (1.0 / 32.0)), 0.0)
    return inner, weight, 1.0 / jnp.sum(weight, axis=-1, keepdims=True)


def attention_kernel(heads, place_ref, bound_ref, qkv_ref, mixed_ref):
    n_q = heads * FK
    key = qkv_ref[:, n_q : 2 * n_q]
    queries = [head_lanes(qkv_ref[:, :n_q], h) for h in range(heads)]
    bound = bound_ref[...]
    for first in range(0, qkv_ref.shape[0], BLOCK):
        seen = bound <= place_ref[first : first + BLOCK]
        for h in range(heads):
            _, weight, scale = weights_of(queries[h][first : first + BLOCK], key, seen)
            value = qkv_ref[:, 2 * n_q + h * DV : 2 * n_q + (h + 1) * DV]
            mixed_ref[first : first + BLOCK, h * DV : (h + 1) * DV] = dot(
                (weight * scale).astype(BF), value
            ).astype(BF)


def cost(flops):
    return pl.CostEstimate(flops=flops, bytes_accessed=2**21, transcendentals=0)


def attention(place, bound, qkv):
    heads = (qkv.shape[1] // (2 * FK + DV))
    return pl.pallas_call(
        functools.partial(attention_kernel, heads),
        out_shape=jax.ShapeDtypeStruct((qkv.shape[0], heads * DV), BF),
        compiler_params=pltpu.CompilerParams(vmem_limit_bytes=32 * 2**20),
        cost_estimate=cost(qkv.shape[0] * qkv.shape[0] * heads * 2 * (2 * FK + DV) * 16),
        name="attention",
    )(place, bound, qkv)


def attention_back_kernel(heads, start, last, *refs):
    if last:
        place_ref, bound_ref, qkv_ref, d_mixed_ref, query_ref, total_ref, out_ref = refs
    else:
        place_ref, bound_ref, qkv_ref, d_mixed_ref, query_ref, total_ref = refs
    n_q = heads * FK
    key = qkv_ref[:, n_q : 2 * n_q]
    keys = [head_lanes(key, h) for h in range(heads)]
    bound = bound_ref[...]
    rows = d_mixed_ref.shape[0]
    d_key = 0.0
    d_values = [0.0] * heads
    for first in range(0, rows, BLOCK):
        here = slice(start + first, start + first + BLOCK)
        seen = bound <= place_ref[here]
        d_query = 0.0
        for h in range(heads):
            query = head_lanes(qkv_ref[here, :n_q], h)
            inner, weight, scale = weights_of(query, key, seen)
            share = weight * scale
            value = qkv_ref[:, 2 * n_q + h * DV : 2 * n_q + (h + 1) * DV]
            d_out = d_mixed_ref[first : first + BLOCK, h * DV : (h + 1) * DV]
            d_share = dot_nt(d_out, value)
            row = jnp.sum(d_share * share, axis=-1, keepdims=True)
            d_inner = jnp.where(
                seen, (d_share - row) * scale * (0.25 + inner * (1.0 / 16.0)), 0.0
            ).astype(BF)
            d_query = d_query + dot(d_inner, keys[h])
            d_key = d_key + dot_tn(d_inner, query)
            d_values[h] = d_values[h] + dot_tn(share.astype(BF), d_out)
        if last:
            out_ref[here, :n_q] = d_query.astype(BF)
        else:
            query_ref[first : first + BLOCK] = d_query.astype(BF)
    if last:
        out_ref[:start, :n_q] = query_ref[...]
        out_ref[:, n_q : 2 * n_q] = (d_key + total_ref[:, heads * DV :]).astype(BF)
        for h in range(heads):
            out_ref[:, 2 * n_q + h * DV : 2 * n_q + (h + 1) * DV] = (
                d_values[h] + total_ref[:, h * DV : (h + 1) * DV]
            ).astype(BF)
    else:
        total_ref[:, heads * DV :] = d_key
        for h in range(heads):
            total_ref[:, h * DV : (h + 1) * DV] = d_values[h]


def attention_back(place, bound, qkv, d_mixed, start, before):
    heads = (qkv.shape[1] // (2 * FK + DV))
    n_q = heads * FK
    rows = d_mixed.shape[0]
    last = before is not None
    if last:
        shape = jax.ShapeDtypeStruct(qkv.shape, BF)
    else:
        shape = (
            jax.ShapeDtypeStruct((rows, n_q), BF),
            jax.ShapeDtypeStruct((qkv.shape[0], n_q + heads * DV), F32),
        )
    return pl.pallas_call(
        functools.partial(attention_back_kernel, heads, start, last),
        out_shape=shape,
        compiler_params=pltpu.CompilerParams(vmem_limit_bytes=40 * 2**20),
        cost_estimate=cost(rows * qkv.shape[0] * heads * 2 * (6 * FK + 2 * DV)),
        name="attention_back",
    )(place, bound, qkv, d_mixed, *(before or ()))


def norm_kernel(inputs_ref, gain_ref, normed_ref, scale_ref):
    values = inputs_ref[...].astype(F32)
    scale = lax.rsqrt(jnp.mean(values * values, axis=-1, keepdims=True) + EPSILON)
    normed_ref[...] = (values * scale * gain_ref[...]).astype(BF)
    scale_ref[...] = scale


def norm(inputs, gain):
    return pl.pallas_call(
        norm_kernel,
        out_shape=(
            jax.ShapeDtypeStruct(inputs.shape, BF),
            jax.ShapeDtypeStruct((inputs.shape[0], 1), F32),
        ),
        compiler_params=pltpu.CompilerParams(vmem_limit_bytes=16 * 2**20),
        name="norm",
    )(inputs, gain[None, :])


def after(value, *others):
    return lax.optimization_barrier((value, *others))[0]


def along(value, pairs):
    return lax.ppermute(value, "mp", pairs)


def on_device(
    tokens,
    lengths,
    w_query,
    w_key,
    w_value,
    w_out,
    w_gate,
    w_up,
    w_down,
    gain_attn,
    gain_mlp,
    out_cotangent,
):
    shard = tokens.shape[0]
    width = tokens.shape[1]
    heads = w_query.shape[1] // FK
    n_q = w_query.shape[1]
    n_dp = lax.axis_size("dp")
    block = width // n_dp
    bits = [1 << b for b in range(n_dp.bit_length() - 1)]
    me_mp = lax.axis_index("mp")
    me_dp = lax.axis_index("dp")
    is_middle = (me_mp == 1) | (me_mp == 2)
    chunk_ids = [
        me_mp,
        me_mp ^ 1,
        jnp.where(is_middle, me_mp ^ 3, me_mp ^ 2),
        jnp.where(is_middle, me_mp ^ 2, me_mp ^ 3),
    ]
    places = jnp.concatenate([c * shard + jnp.arange(shard, dtype=jnp.int32) for c in chunk_ids])
    bound = jnp.where(places < lengths[0], places, UNSEEN)[None, :]
    places = places[:, None]

    order_one = bits[1:]
    order_two = order_one[::-1]
    even_slots = [2, 6, 4, 0] if n_dp == 8 else list(range(0, n_dp, 2))
    second_slots = [0, 2, 6, 4] if n_dp == 8 else list(range(0, n_dp, 2))

    def rows_of(array, slot):
        return array[slot * shard : (slot + 1) * shard]

    def exchange(outward, inward):
        return along(jnp.where(is_middle, outward, inward), PAIRS)

    def swap_dp(value, bit):
        return lax.ppermute(value, "dp", [(i, i ^ bit) for i in range(n_dp)])

    def both_rows(array):
        return jnp.concatenate([array, swap_dp(array, 1)], axis=0)

    def take(array, held, slots, axis, size=None):
        size = size or block
        at = [held.index(k) for k in slots]
        if at == list(range(at[0], at[0] + len(at))):
            return lax.slice_in_dim(array, at[0] * size, (at[-1] + 1) * size, axis=axis)
        return jnp.concatenate(
            [lax.slice_in_dim(array, i * size, (i + 1) * size, axis=axis) for i in at], axis=axis
        )

    def column_blocks(array):
        def pick(slots):
            return jnp.concatenate(
                [
                    lax.dynamic_slice_in_dim(array, (me_dp ^ k) * block, block, axis=1)
                    for k in slots
                ],
                axis=1,
            )

        theirs = swap_dp(pick([k ^ 1 for k in even_slots]), 1)
        return jnp.concatenate([pick(even_slots), theirs], axis=0)

    half = block // 2

    def half_picks(array):
        def pick(odd):
            cuts = [(k, 0) for k in even_slots] + [(k, half) for k in second_slots]
            return jnp.concatenate(
                [
                    lax.dynamic_slice_in_dim(
                        array, (me_dp ^ k ^ odd) * block + shift, half, axis=1
                    )
                    for k, shift in cuts
                ],
                axis=1,
            )

        return pick(0), swap_dp(pick(1), 1)

    def half_columns(array):
        return jnp.concatenate(half_picks(array), axis=0)

    def half_sums(columns, other, side, stage, gots):
        order = (order_one, order_two)[side]
        held = (even_slots, second_slots)[side]
        base = side * len(even_slots) * half
        cut = lax.slice_in_dim(columns, base, base + len(even_slots) * half, axis=1)
        slots = away_slots(order, stage)
        total = dot_tn(take(cut, held, slots, 1, half), other)
        for earlier, got in enumerate(gots):
            there = [k ^ order[earlier] for k in away_slots(order, earlier)]
            total = total + take(got, there, slots, 0, half).astype(F32)
        return total

    def send_halves(pair_of_halves, stage):
        return [
            swap_dp(part, order[stage])
            for part, order in zip(pair_of_halves, (order_one, order_two))
        ]

    def final_product(columns, other):
        at = (len(even_slots) - 1) * half
        if even_slots[-1] == second_slots[0] == 0:
            total = dot_tn(lax.slice_in_dim(columns, at, at + block, axis=1), other)
            return total[:half], total[half:]
        return [half_sums(columns, other, side, len(order_one), []) for side in (0, 1)]

    def final_rows(parts, gots):
        parts = list(parts)
        for side, order in enumerate((order_one, order_two)):
            for stage, got in enumerate(gots[side]):
                there = [k ^ order[stage] for k in away_slots(order, stage)]
                parts[side] = parts[side] + take(got, there, [0], 0, half).astype(F32)
        return jnp.concatenate(parts, axis=0)

    def away_slots(order, stage):
        if stage == len(order):
            return [0]
        return [
            k for k in even_slots if k & order[stage] and not any(k & b for b in order[:stage])
        ]

    def block_sums(blocks, other, axis, order, gots, total=None):
        slots = away_slots(order, len(gots))
        picked = take(blocks, even_slots, slots, 1)
        if total is None:
            total = dot_tn(picked, other) if axis == 0 else dot_tn(other, picked)
        for stage, got in enumerate(gots):
            held = [k ^ order[stage] for k in away_slots(order, stage)]
            total = total + take(got, held, slots, axis).astype(F32)
        return total

    def pass_on(sums, gots):
        blocks, other, axis, order = sums
        while True:
            go = block_sums(*sums, gots).astype(BF)
            gots.append(swap_dp(go, order[len(gots)]))
            if len(gots) == len(order):
                return go

    inputs = tokens.astype(F32)
    normed, scale_one = norm(tokens, gain_attn)
    one = along(normed, PAIRS)
    near = along(normed, MIDDLE)
    w_qkv = jnp.concatenate([w_query, w_key, w_value], axis=1)
    qkv_0 = dot(normed, w_qkv).astype(BF)
    near, one = after(near, qkv_0), after(one, qkv_0)
    far = along(one, MIDDLE)
    two = exchange(near, out_cotangent)
    qkv_1 = dot(one, w_qkv).astype(BF)
    cot_near = along(after(out_cotangent, qkv_1), MIDDLE)
    far, two = after(far, qkv_1), after(two, qkv_1)
    three = along(far, OUTWARD)
    cot_1 = two
    slot_2 = jnp.where(is_middle, near, two)
    qkv_2 = dot(slot_2, w_qkv).astype(BF)
    cot_far = along(after(cot_1, slot_2), MIDDLE)
    three = after(three, qkv_2, cot_near)
    slot_3 = jnp.where(is_middle, far, three)
    qkv_3 = dot(slot_3, w_qkv).astype(BF)
    normed_full = jnp.concatenate([normed, one, slot_2, slot_3], axis=0)
    qkv = jnp.concatenate([qkv_0, qkv_1, qkv_2, qkv_3], axis=0)
    mixed = attention(places, bound, qkv)

    third = dot(rows_of(mixed, 3), w_out).astype(BF)
    edge = exchange(out_cotangent, third)
    second = dot(after(rows_of(mixed, 2), third), w_out).astype(BF)
    first = dot(after(rows_of(mixed, 1), third), w_out)
    zeroth = dot(after(rows_of(mixed, 0), third), w_out)
    edge = after(edge, second, first, zeroth)
    across = along(third + edge, MIDDLE)
    edge_two = exchange(cot_near, after(second, edge))
    cot_1 = jnp.where(is_middle, cot_1, edge)
    mixed_both = both_rows(after(mixed, edge))
    normed_blocks = column_blocks(after(normed_full, edge))
    across, edge_two, cot_far = (
        after(across, mixed_both, normed_blocks, cot_1),
        after(edge_two, mixed_both, normed_blocks, cot_1),
        after(cot_far, mixed_both, normed_blocks, cot_1),
    )
    pair = along((first + across.astype(F32)).astype(BF), PAIRS)
    middle = along(second + edge_two, MIDDLE)
    cot_2 = jnp.where(is_middle, cot_near, edge_two)
    cot_three = along(after(cot_far, cot_2), OUTWARD)
    cot_012 = jnp.concatenate([out_cotangent, cot_1, cot_2], axis=0)
    back_012 = dot_nt(cot_012, w_down).astype(BF)
    cot_early = half_picks(cot_012)
    pair, middle = after(pair, back_012), after(middle, back_012)
    resid = inputs + (zeroth + pair.astype(F32) + middle.astype(F32))

    scale_two = lax.rsqrt(jnp.mean(resid * resid, axis=-1, keepdims=True) + EPSILON)
    normed_two = (resid * scale_two * gain_mlp).astype(BF)

    units = w_gate.shape[1]
    wide = -(-units // LANES) * LANES

    def feed(slot_rows, back):
        gate = dot(slot_rows, w_gate)
        upward = dot(slot_rows, w_up)
        sig = jax.nn.sigmoid(gate)
        active = gate * sig
        back = back.astype(F32)
        hid = (active * upward).astype(BF)
        d_g = (back * upward * sig * (1.0 + gate * (1.0 - sig))).astype(BF)
        d_u = (back * active).astype(BF)
        d_both = jnp.concatenate(
            [jnp.pad(d, ((0, 0), (0, wide - units))) for d in (d_g, d_u)], axis=1
        )
        return hid, lax.optimization_barrier(d_both)

    def unfeed(fed):
        d_both = fed[1]
        return dot_nt(d_both[:, :units], w_gate) + dot_nt(d_both[:, wide : wide + units], w_up)

    one = along(normed_two, PAIRS)
    near = along(normed_two, MIDDLE)
    fed_0 = feed(normed_two, rows_of(back_012, 0))
    part_0 = unfeed(fed_0)
    near, one = after(near, part_0), after(one, part_0)
    two = along(near, OUTWARD)
    far = along(one, MIDDLE)
    fed_1 = feed(one, rows_of(back_012, 1))
    part_1 = unfeed(fed_1)
    out_1 = dot(fed_1[0], w_down)
    cot_3 = jnp.where(is_middle, cot_far, after(cot_three, one))
    back_3 = dot_nt(cot_3, w_down).astype(BF)
    far, two = after(far, part_1, out_1, back_3), after(two, part_1, out_1, back_3)
    three = exchange(far, out_1.astype(BF))
    cot_full = jnp.concatenate([out_cotangent, cot_1, cot_2, after(cot_3, two)], axis=0)
    slot_2 = jnp.where(is_middle, near, two)
    fed_2 = feed(slot_2, rows_of(back_012, 2))
    part_2 = unfeed(fed_2).astype(BF)
    three = after(three, part_2)
    out_in = three
    slot_3 = jnp.where(is_middle, far, three)
    fed_3 = feed(slot_3, back_3)
    third = unfeed(fed_3).astype(BF)

    edge = along(third, INWARD)
    hidden_s, d_feed_s = zip(fed_0, fed_1, fed_2, fed_3)
    hidden_both = both_rows(after(jnp.concatenate(hidden_s, axis=0), third))
    second_full = jnp.concatenate([normed_two, one, slot_2, slot_3], axis=0)
    cot_late = half_picks(after(cot_3, third))
    cot_columns = jnp.concatenate([cot_early[0], cot_late[0], cot_early[1], cot_late[1]], axis=0)
    down_pay = [half_sums(cot_columns, hidden_both, side, 0, []).astype(BF) for side in (0, 1)]
    down_got = send_halves(down_pay, 0)
    edge = after(edge, *down_pay)
    across = along(third + edge, MIDDLE)
    edge_two = along(after(part_2, edge), INWARD)
    second_columns = half_columns(after(second_full, edge))
    d_feed = jnp.concatenate(d_feed_s, axis=0)
    feed_both = both_rows(after(d_feed, edge))
    feed_pay = [half_sums(second_columns, feed_both, side, 0, []).astype(BF) for side in (0, 1)]
    across, edge_two = after(across, *feed_pay), after(edge_two, *feed_pay)
    pair = along((part_1 + across.astype(F32)).astype(BF), PAIRS)
    middle = along(part_2 + edge_two, MIDDLE)
    down_got = [after(g, *feed_pay) for g in down_got]
    feed_got = send_halves([after(p, *down_got) for p in feed_pay], 0)
    out_3 = dot(after(fed_3[0], across), w_down).astype(BF)
    pair = after(pair, out_3)
    d_normed_two = part_0 + pair.astype(F32) + middle.astype(F32)
    weighted_two = d_normed_two * gain_mlp
    d_resid = (
        out_cotangent.astype(F32)
        + scale_two * weighted_two
        - resid * scale_two**3 * jnp.mean(weighted_two * resid, axis=-1, keepdims=True)
    )
    d_attn = d_resid.astype(BF)

    one = along(d_attn, PAIRS)
    near = along(d_attn, MIDDLE)
    gain_two_part = jnp.sum(d_normed_two * resid * scale_two, axis=0)
    out_2 = dot(after(fed_2[0], d_attn), w_down).astype(BF)
    out_0 = dot(after(fed_0[0], d_attn), w_down)
    feed_stays = final_product(after(second_columns, d_attn), feed_both)
    down_stays = final_product(after(cot_columns, d_attn), hidden_both)
    early = (gain_two_part, out_0, out_2)
    near, one = after(near, *early), after(one, *early)
    far = along(one, MIDDLE)
    two = exchange(near, out_3)
    d_mixed_0 = dot_nt(after(d_attn, one), w_out).astype(BF)
    d_mixed_1 = dot_nt(after(one, d_mixed_0), w_out).astype(BF)
    far, two = after(far, d_mixed_1), after(two, d_mixed_1)
    three = exchange(far, out_2)
    slot_2 = jnp.where(is_middle, near, two)
    d_mixed_2 = dot_nt(slot_2, w_out).astype(BF)
    out_across = along(out_3 + after(two, d_mixed_2), MIDDLE)
    before = attention_back(
        places, bound, qkv, jnp.concatenate([d_mixed_0, d_mixed_1, d_mixed_2], axis=0), 0, None
    )
    feed_got = [after(g, d_mixed_1) for g in feed_got]
    feed_gots = [[g] for g in feed_got]
    down_gots = [[g] for g in down_got]
    rests = []
    for stage in range(1, len(order_one)):
        rest = [
            jnp.concatenate(
                [
                    half_sums(second_columns, feed_both, side, stage, feed_gots[side]),
                    half_sums(cot_columns, hidden_both, side, stage, down_gots[side]),
                ],
                axis=1,
            ).astype(BF)
            for side in (0, 1)
        ]
        rest_got = [after(got, before[0]) for got in send_halves(rest, stage)]
        rests.append(rest_got)
        for side, got in enumerate(rest_got):
            feed_gots[side].append(got[:, : d_feed.shape[1]])
            down_gots[side].append(got[:, d_feed.shape[1] :])
    three = after(three, before[0])
    slot_3 = jnp.where(is_middle, far, three)
    d_mixed_3 = dot_nt(slot_3, w_out).astype(BF)
    d_qkv = attention_back(places, bound, qkv, d_mixed_3, 3 * shard, before)

    third = dot_nt(rows_of(d_qkv, 3), w_qkv).astype(BF)
    edge = along(third, INWARD)
    qkv_both = both_rows(after(d_qkv, third))
    second = dot_nt(after(rows_of(d_qkv, 2), third), w_qkv).astype(BF)
    first = dot_nt(after(rows_of(d_qkv, 1), third), w_qkv)
    zeroth = dot_nt(after(rows_of(d_qkv, 0), third), w_qkv)
    out_middle = along(after(out_2 + three, second), MIDDLE)
    out_sum = (out_1 + after(out_across, second).astype(F32)).astype(BF)
    d_normed_part = jnp.concatenate([zeroth, first, second.astype(F32), third.astype(F32)], axis=0)
    gain_one_part = jnp.sum(d_normed_part * normed_full.astype(F32), axis=0)
    gains = jnp.stack([gain_one_part / gain_attn, gain_two_part])
    gains = gains + swap_dp(gains, bits[0])
    gains_got = swap_dp(gains, bits[1])
    of_qkv = (normed_blocks, after(qkv_both, gains), 0, order_one)
    qkv_go = block_sums(*of_qkv, []).astype(BF)
    qkv_got = swap_dp(qkv_go, order_one[0])
    edge = after(edge, out_sum, gains, *rest_got)
    across = along(third + edge, MIDDLE)
    edge_two = exchange(out_sum, after(second, edge))
    gains = gains + after(gains_got, edge, qkv_go)
    for bit in bits[2:]:
        gains = gains + swap_dp(gains, bit)
    attn_full = jnp.concatenate([d_attn, one, slot_2, slot_3], axis=0)
    attn_blocks = column_blocks(after(attn_full, third))
    of_out = (attn_blocks, mixed_both, 1, order_two)
    out_go = block_sums(*of_out, []).astype(BF)
    out_got = swap_dp(out_go, order_two[0])
    across, edge_two = after(across, out_go), after(edge_two, out_go)
    gains_there = gains
    gains = gains.astype(BF)
    pair = along(
        jnp.concatenate([(first + across.astype(F32)).astype(BF), gains], axis=0), PAIRS
    )
    middle = along(second + edge_two, MIDDLE)
    qkv_gots = [after(qkv_got, across)]
    qkv_mid = pass_on(of_qkv, qkv_gots)
    out_gots = [after(out_got, across)]
    out_back = pass_on(of_out, out_gots)
    gains = gains.astype(F32) + pair[shard:].astype(F32)
    gains = gains + along(gains, [(i, i ^ 2) for i in range(4)])
    pair = pair[:shard]
    down_late = [
        [after(down_gots[side][0], qkv_mid)]
        + [after(r[side], qkv_mid)[:, d_feed.shape[1] :] for r in rests]
        for side in (0, 1)
    ]
    grad_down = final_rows(down_stays, down_late).T
    feed_late = [
        [after(feed_gots[side][0], qkv_go)]
        + [after(r[side], qkv_go)[:, : d_feed.shape[1]] for r in rests]
        for side in (0, 1)
    ]
    grad_feed = final_rows(feed_stays, feed_late)
    qkv_stays = dot_tn(take(after(of_qkv[0], qkv_mid), even_slots, [0], 1), of_qkv[1])
    out_stays = dot_tn(mixed_both, take(after(attn_blocks, qkv_mid), even_slots, [0], 1))
    grad_qkv = block_sums(*of_qkv, qkv_gots, qkv_stays)
    grad_out = block_sums(*of_out, out_gots, out_stays)
    out_rest = jnp.where(
        is_middle, out_in.astype(F32) + after(out_middle, across).astype(F32), edge_two.astype(F32)
    )
    outputs = (resid + (out_0 + out_rest)).astype(BF)
    d_normed = zeroth + pair.astype(F32) + middle.astype(F32)
    weighted_one = d_normed * gain_attn
    grad_tokens = (
        d_resid
        + scale_one * weighted_one
        - inputs * scale_one**3 * jnp.mean(weighted_one * inputs, axis=-1, keepdims=True)
    )
    return (
        outputs,
        grad_tokens,
        grad_qkv[:, :n_q],
        grad_qkv[:, n_q : 2 * n_q],
        grad_qkv[:, 2 * n_q :],
        grad_out,
        grad_feed[:, :units],
        grad_feed[:, wide : wide + units],
        grad_down,
        gains[0],
        gains[1],
    )


def solution(mesh):
    return jax.shard_map(
        on_device,
        mesh=mesh,
        in_specs=(
            P(("dp", "mp"), None),
            P("dp"),
            P(None, "mp"),
            P(None, "mp"),
            P(None, "mp"),
            P("mp", None),
            P(None, "mp"),
            P(None, "mp"),
            P("mp", None),
            P(),
            P(),
            P(("dp", "mp"), None),
        ),
        out_specs=(
            P(("dp", "mp"), None),
            P(("dp", "mp"), None),
            P("dp", "mp"),
            P("dp", "mp"),
            P("dp", "mp"),
            P("mp", "dp"),
            P("dp", "mp"),
            P("dp", "mp"),
            P("mp", "dp"),
            P(),
            P(),
        ),
        check_vma=False,
    )
```

```python
import functools

import jax
import jax.numpy as jnp
from jax import lax
from jax.experimental import pallas as pl
from jax.experimental.pallas import tpu as pltpu
from jax.sharding import PartitionSpec as P

FK = 16
DV = 128
BF = jnp.bfloat16
F32 = jnp.float32
EPSILON = 1e-06
BLOCK = 128
UNSEEN = 1 << 24
LANES = 128

PAIRS = [(0, 1), (1, 0), (2, 3), (3, 2)]
MIDDLE = [(1, 2), (2, 1)]
OUTWARD = [(2, 3), (1, 0)]
INWARD = [(3, 2), (0, 1)]


def dot(left, right):
    return jnp.dot(left, right, preferred_element_type=F32)


def dot_nt(left, right):
    return lax.dot_general(left, right, (((1,), (1,)), ((), ())), preferred_element_type=F32)


def dot_tn(left, right):
    return lax.dot_general(left, right, (((0,), (0,)), ((), ())), preferred_element_type=F32)


def head_lanes(array, head):
    lane = lax.broadcasted_iota(jnp.int32, array.shape, 1) // FK
    return jnp.where(lane == head, array.astype(F32), 0.0).astype(BF)


def weights_of(query, key, seen):
    inner = dot_nt(query, key)
    weight = jnp.where(seen, 1.0 + inner * (0.25 + inner * (1.0 / 32.0)), 0.0)
    return inner, weight, 1.0 / jnp.sum(weight, axis=-1, keepdims=True)


def attention_kernel(heads, place_ref, bound_ref, qkv_ref, mixed_ref):
    n_q = heads * FK
    key = qkv_ref[:, n_q : 2 * n_q]
    queries = [head_lanes(qkv_ref[:, :n_q], h) for h in range(heads)]
    bound = bound_ref[...]
    for first in range(0, qkv_ref.shape[0], BLOCK):
        seen = bound <= place_ref[first : first + BLOCK]
        for h in range(heads):
            _, weight, scale = weights_of(queries[h][first : first + BLOCK], key, seen)
            value = qkv_ref[:, 2 * n_q + h * DV : 2 * n_q + (h + 1) * DV]
            mixed_ref[first : first + BLOCK, h * DV : (h + 1) * DV] = dot(
                (weight * scale).astype(BF), value
            ).astype(BF)


def cost(flops):
    return pl.CostEstimate(flops=flops, bytes_accessed=2**21, transcendentals=0)


def attention(place, bound, qkv):
    heads = (qkv.shape[1] // (2 * FK + DV))
    return pl.pallas_call(
        functools.partial(attention_kernel, heads),
        out_shape=jax.ShapeDtypeStruct((qkv.shape[0], heads * DV), BF),
        compiler_params=pltpu.CompilerParams(vmem_limit_bytes=32 * 2**20),
        cost_estimate=cost(qkv.shape[0] * qkv.shape[0] * heads * 2 * (2 * FK + DV) * 16),
        name="attention",
    )(place, bound, qkv)


def attention_back_kernel(heads, start, last, *refs):
    if last:
        place_ref, bound_ref, qkv_ref, d_mixed_ref, query_ref, total_ref, out_ref = refs
    else:
        place_ref, bound_ref, qkv_ref, d_mixed_ref, query_ref, total_ref = refs
    n_q = heads * FK
    key = qkv_ref[:, n_q : 2 * n_q]
    keys = [head_lanes(key, h) for h in range(heads)]
    bound = bound_ref[...]
    rows = d_mixed_ref.shape[0]
    d_key = 0.0
    d_values = [0.0] * heads
    for first in range(0, rows, BLOCK):
        here = slice(start + first, start + first + BLOCK)
        seen = bound <= place_ref[here]
        d_query = 0.0
        for h in range(heads):
            query = head_lanes(qkv_ref[here, :n_q], h)
            inner, weight, scale = weights_of(query, key, seen)
            share = weight * scale
            value = qkv_ref[:, 2 * n_q + h * DV : 2 * n_q + (h + 1) * DV]
            d_out = d_mixed_ref[first : first + BLOCK, h * DV : (h + 1) * DV]
            d_share = dot_nt(d_out, value)
            row = jnp.sum(d_share * share, axis=-1, keepdims=True)
            d_inner = jnp.where(
                seen, (d_share - row) * scale * (0.25 + inner * (1.0 / 16.0)), 0.0
            ).astype(BF)
            d_query = d_query + dot(d_inner, keys[h])
            d_key = d_key + dot_tn(d_inner, query)
            d_values[h] = d_values[h] + dot_tn(share.astype(BF), d_out)
        if last:
            out_ref[here, :n_q] = d_query.astype(BF)
        else:
            query_ref[first : first + BLOCK] = d_query.astype(BF)
    if last:
        out_ref[:start, :n_q] = query_ref[...]
        out_ref[:, n_q : 2 * n_q] = (d_key + total_ref[:, heads * DV :]).astype(BF)
        for h in range(heads):
            out_ref[:, 2 * n_q + h * DV : 2 * n_q + (h + 1) * DV] = (
                d_values[h] + total_ref[:, h * DV : (h + 1) * DV]
            ).astype(BF)
    else:
        total_ref[:, heads * DV :] = d_key
        for h in range(heads):
            total_ref[:, h * DV : (h + 1) * DV] = d_values[h]


def attention_back(place, bound, qkv, d_mixed, start, before):
    heads = (qkv.shape[1] // (2 * FK + DV))
    n_q = heads * FK
    rows = d_mixed.shape[0]
    last = before is not None
    if last:
        shape = jax.ShapeDtypeStruct(qkv.shape, BF)
    else:
        shape = (
            jax.ShapeDtypeStruct((rows, n_q), BF),
            jax.ShapeDtypeStruct((qkv.shape[0], n_q + heads * DV), F32),
        )
    return pl.pallas_call(
        functools.partial(attention_back_kernel, heads, start, last),
        out_shape=shape,
        compiler_params=pltpu.CompilerParams(vmem_limit_bytes=40 * 2**20),
        cost_estimate=cost(rows * qkv.shape[0] * heads * 2 * (6 * FK + 2 * DV)),
        name="attention_back",
    )(place, bound, qkv, d_mixed, *(before or ()))


def norm_kernel(inputs_ref, gain_ref, normed_ref, scale_ref):
    values = inputs_ref[...].astype(F32)
    scale = lax.rsqrt(jnp.mean(values * values, axis=-1, keepdims=True) + EPSILON)
    normed_ref[...] = (values * scale * gain_ref[...]).astype(BF)
    scale_ref[...] = scale


def norm(inputs, gain):
    return pl.pallas_call(
        norm_kernel,
        out_shape=(
            jax.ShapeDtypeStruct(inputs.shape, BF),
            jax.ShapeDtypeStruct((inputs.shape[0], 1), F32),
        ),
        compiler_params=pltpu.CompilerParams(vmem_limit_bytes=16 * 2**20),
        name="norm",
    )(inputs, gain[None, :])


def after(value, *others):
    return lax.optimization_barrier((value, *others))[0]


def along(value, pairs):
    return lax.ppermute(value, "mp", pairs)


def on_device(
    tokens,
    lengths,
    w_query,
    w_key,
    w_value,
    w_out,
    w_gate,
    w_up,
    w_down,
    gain_attn,
    gain_mlp,
    out_cotangent,
):
    shard = tokens.shape[0]
    width = tokens.shape[1]
    heads = w_query.shape[1] // FK
    n_q = w_query.shape[1]
    n_dp = lax.axis_size("dp")
    block = width // n_dp
    bits = [1 << b for b in range(n_dp.bit_length() - 1)]
    me_mp = lax.axis_index("mp")
    me_dp = lax.axis_index("dp")
    is_middle = (me_mp == 1) | (me_mp == 2)
    chunk_ids = [
        me_mp,
        me_mp ^ 1,
        jnp.where(is_middle, me_mp ^ 3, me_mp ^ 2),
        jnp.where(is_middle, me_mp ^ 2, me_mp ^ 3),
    ]
    places = jnp.concatenate([c * shard + jnp.arange(shard, dtype=jnp.int32) for c in chunk_ids])
    bound = jnp.where(places < lengths[0], places, UNSEEN)[None, :]
    places = places[:, None]

    order_one = bits[1:]
    order_two = order_one[::-1]
    even_slots = [2, 6, 4, 0] if n_dp == 8 else list(range(0, n_dp, 2))
    second_slots = [0, 2, 6, 4] if n_dp == 8 else list(range(0, n_dp, 2))

    def rows_of(array, slot):
        return array[slot * shard : (slot + 1) * shard]

    def exchange(outward, inward):
        return along(jnp.where(is_middle, outward, inward), PAIRS)

    def swap_dp(value, bit):
        return lax.ppermute(value, "dp", [(i, i ^ bit) for i in range(n_dp)])

    def both_rows(array):
        return jnp.concatenate([array, swap_dp(array, 1)], axis=0)

    def take(array, held, slots, axis, size=None):
        size = size or block
        at = [held.index(k) for k in slots]
        if at == list(range(at[0], at[0] + len(at))):
            return lax.slice_in_dim(array, at[0] * size, (at[-1] + 1) * size, axis=axis)
        return jnp.concatenate(
            [lax.slice_in_dim(array, i * size, (i + 1) * size, axis=axis) for i in at], axis=axis
        )

    def column_blocks(array):
        def pick(slots):
            return jnp.concatenate(
                [
                    lax.dynamic_slice_in_dim(array, (me_dp ^ k) * block, block, axis=1)
                    for k in slots
                ],
                axis=1,
            )

        theirs = swap_dp(pick([k ^ 1 for k in even_slots]), 1)
        return jnp.concatenate([pick(even_slots), theirs], axis=0)

    half = block // 2

    def half_picks(array):
        def pick(odd):
            cuts = [(k, 0) for k in even_slots] + [(k, half) for k in second_slots]
            return jnp.concatenate(
                [
                    lax.dynamic_slice_in_dim(
                        array, (me_dp ^ k ^ odd) * block + shift, half, axis=1
                    )
                    for k, shift in cuts
                ],
                axis=1,
            )

        return pick(0), swap_dp(pick(1), 1)

    def half_columns(array):
        return jnp.concatenate(half_picks(array), axis=0)

    def half_sums(columns, other, side, stage, gots):
        order = (order_one, order_two)[side]
        held = (even_slots, second_slots)[side]
        base = side * len(even_slots) * half
        cut = lax.slice_in_dim(columns, base, base + len(even_slots) * half, axis=1)
        slots = away_slots(order, stage)
        total = dot_tn(take(cut, held, slots, 1, half), other)
        for earlier, got in enumerate(gots):
            there = [k ^ order[earlier] for k in away_slots(order, earlier)]
            total = total + take(got, there, slots, 0, half).astype(F32)
        return total

    def send_halves(pair_of_halves, stage):
        return [
            swap_dp(part, order[stage])
            for part, order in zip(pair_of_halves, (order_one, order_two))
        ]

    def final_product(columns, other):
        at = (len(even_slots) - 1) * half
        if even_slots[-1] == second_slots[0] == 0:
            total = dot_tn(lax.slice_in_dim(columns, at, at + block, axis=1), other)
            return total[:half], total[half:]
        return [half_sums(columns, other, side, len(order_one), []) for side in (0, 1)]

    def final_rows(parts, gots):
        parts = list(parts)
        for side, order in enumerate((order_one, order_two)):
            for stage, got in enumerate(gots[side]):
                there = [k ^ order[stage] for k in away_slots(order, stage)]
                parts[side] = parts[side] + take(got, there, [0], 0, half).astype(F32)
        return jnp.concatenate(parts, axis=0)

    def away_slots(order, stage):
        if stage == len(order):
            return [0]
        return [
            k for k in even_slots if k & order[stage] and not any(k & b for b in order[:stage])
        ]

    def block_sums(blocks, other, axis, order, gots, total=None):
        slots = away_slots(order, len(gots))
        picked = take(blocks, even_slots, slots, 1)
        if total is None:
            total = dot_tn(picked, other) if axis == 0 else dot_tn(other, picked)
        for stage, got in enumerate(gots):
            held = [k ^ order[stage] for k in away_slots(order, stage)]
            total = total + take(got, held, slots, axis).astype(F32)
        return total

    def pass_on(sums, gots):
        blocks, other, axis, order = sums
        while True:
            go = block_sums(*sums, gots).astype(BF)
            gots.append(swap_dp(go, order[len(gots)]))
            if len(gots) == len(order):
                return go

    inputs = tokens.astype(F32)
    normed, scale_one = norm(tokens, gain_attn)
    one = along(normed, PAIRS)
    near = along(normed, MIDDLE)
    w_qkv = jnp.concatenate([w_query, w_key, w_value], axis=1)
    qkv_0 = dot(normed, w_qkv).astype(BF)
    near, one = after(near, qkv_0), after(one, qkv_0)
    far = along(one, MIDDLE)
    two = exchange(near, out_cotangent)
    qkv_1 = dot(one, w_qkv).astype(BF)
    cot_near = along(after(out_cotangent, qkv_1), MIDDLE)
    far, two = after(far, qkv_1), after(two, qkv_1)
    three = along(far, OUTWARD)
    cot_1 = two
    slot_2 = jnp.where(is_middle, near, two)
    qkv_2 = dot(slot_2, w_qkv).astype(BF)
    cot_far = along(after(cot_1, slot_2), MIDDLE)
    three = after(three, qkv_2, cot_near)
    slot_3 = jnp.where(is_middle, far, three)
    qkv_3 = dot(slot_3, w_qkv).astype(BF)
    normed_full = jnp.concatenate([normed, one, slot_2, slot_3], axis=0)
    qkv = jnp.concatenate([qkv_0, qkv_1, qkv_2, qkv_3], axis=0)
    mixed = attention(places, bound, qkv)

    third = dot(rows_of(mixed, 3), w_out).astype(BF)
    edge = exchange(out_cotangent, third)
    second = dot(after(rows_of(mixed, 2), third), w_out).astype(BF)
    first = dot(after(rows_of(mixed, 1), third), w_out)
    zeroth = dot(after(rows_of(mixed, 0), third), w_out)
    edge = after(edge, second, first, zeroth)
    across = along(third + edge, MIDDLE)
    edge_two = exchange(cot_near, after(second, edge))
    cot_1 = jnp.where(is_middle, cot_1, edge)
    mixed_both = both_rows(after(mixed, edge))
    normed_blocks = column_blocks(after(normed_full, edge))
    across, edge_two, cot_far = (
        after(across, mixed_both, normed_blocks, cot_1),
        after(edge_two, mixed_both, normed_blocks, cot_1),
        after(cot_far, mixed_both, normed_blocks, cot_1),
    )
    pair = along((first + across.astype(F32)).astype(BF), PAIRS)
    middle = along(second + edge_two, MIDDLE)
    cot_2 = jnp.where(is_middle, cot_near, edge_two)
    cot_three = along(after(cot_far, cot_2), OUTWARD)
    cot_012 = jnp.concatenate([out_cotangent, cot_1, cot_2], axis=0)
    back_012 = dot_nt(cot_012, w_down).astype(BF)
    cot_early = half_picks(cot_012)
    pair, middle = after(pair, back_012), after(middle, back_012)
    resid = inputs + (zeroth + pair.astype(F32) + middle.astype(F32))

    scale_two = lax.rsqrt(jnp.mean(resid * resid, axis=-1, keepdims=True) + EPSILON)
    normed_two = (resid * scale_two * gain_mlp).astype(BF)

    units = w_gate.shape[1]
    wide = -(-units // LANES) * LANES

    def feed(slot_rows, back):
        gate = dot(slot_rows, w_gate)
        upward = dot(slot_rows, w_up)
        sig = jax.nn.sigmoid(gate)
        active = gate * sig
        back = back.astype(F32)
        hid = (active * upward).astype(BF)
        d_g = (back * upward * sig * (1.0 + gate * (1.0 - sig))).astype(BF)
        d_u = (back * active).astype(BF)
        d_both = jnp.concatenate(
            [jnp.pad(d, ((0, 0), (0, wide - units))) for d in (d_g, d_u)], axis=1
        )
        return hid, lax.optimization_barrier(d_both)

    def unfeed(fed):
        d_both = fed[1]
        return dot_nt(d_both[:, :units], w_gate) + dot_nt(d_both[:, wide : wide + units], w_up)

    one = along(normed_two, PAIRS)
    near = along(normed_two, MIDDLE)
    fed_0 = feed(normed_two, rows_of(back_012, 0))
    part_0 = unfeed(fed_0)
    near, one = after(near, part_0), after(one, part_0)
    two = along(near, OUTWARD)
    far = along(one, MIDDLE)
    fed_1 = feed(one, rows_of(back_012, 1))
    part_1 = unfeed(fed_1)
    out_1 = dot(fed_1[0], w_down)
    cot_3 = jnp.where(is_middle, cot_far, after(cot_three, one))
    back_3 = dot_nt(cot_3, w_down).astype(BF)
    far, two = after(far, part_1, out_1, back_3), after(two, part_1, out_1, back_3)
    payload = jnp.where(is_middle, far, out_1.astype(BF))
    three = along(payload, PAIRS)
    cot_full = jnp.concatenate([out_cotangent, cot_1, cot_2, after(cot_3, two)], axis=0)
    slot_2 = after(jnp.where(is_middle, near, two), payload)
    fed_2 = feed(slot_2, rows_of(back_012, 2))
    part_2 = unfeed(fed_2).astype(BF)
    three = after(three, part_2)
    out_in = three
    slot_3 = jnp.where(is_middle, far, three)
    fed_3 = feed(slot_3, back_3)
    third = unfeed(fed_3).astype(BF)

    edge = along(third, INWARD)
    hidden_s, d_feed_s = zip(fed_0, fed_1, fed_2, fed_3)
    hidden_both = both_rows(after(jnp.concatenate(hidden_s, axis=0), third))
    second_full = jnp.concatenate([normed_two, one, slot_2, slot_3], axis=0)
    cot_late = half_picks(after(cot_3, third))
    cot_columns = jnp.concatenate([cot_early[0], cot_late[0], cot_early[1], cot_late[1]], axis=0)
    down_pay = [half_sums(cot_columns, hidden_both, side, 0, []).astype(BF) for side in (0, 1)]
    down_got = send_halves(down_pay, 0)
    edge = after(edge, *down_pay)
    across = along(third + edge, MIDDLE)
    edge_two = along(after(part_2, edge), INWARD)
    second_columns = half_columns(after(second_full, edge))
    d_feed = jnp.concatenate(d_feed_s, axis=0)
    feed_both = both_rows(after(d_feed, edge))
    feed_pay = [half_sums(second_columns, feed_both, side, 0, []).astype(BF) for side in (0, 1)]
    across, edge_two = after(across, *feed_pay), after(edge_two, *feed_pay)
    pair = along((part_1 + across.astype(F32)).astype(BF), PAIRS)
    middle = along(part_2 + edge_two, MIDDLE)
    down_got = [after(g, *feed_pay) for g in down_got]
    feed_got = send_halves([after(p, *down_got) for p in feed_pay], 0)
    out_3 = dot(after(fed_3[0], across), w_down).astype(BF)
    pair = after(pair, out_3)
    d_normed_two = part_0 + pair.astype(F32) + middle.astype(F32)
    weighted_two = d_normed_two * gain_mlp
    d_resid = (
        out_cotangent.astype(F32)
        + scale_two * weighted_two
        - resid * scale_two**3 * jnp.mean(weighted_two * resid, axis=-1, keepdims=True)
    )
    d_attn = d_resid.astype(BF)

    one = along(d_attn, PAIRS)
    near = along(d_attn, MIDDLE)
    gain_two_part = jnp.sum(d_normed_two * resid * scale_two, axis=0)
    out_2 = dot(after(fed_2[0], d_attn), w_down).astype(BF)
    out_0 = dot(after(fed_0[0], d_attn), w_down)
    feed_stays = final_product(after(second_columns, d_attn), feed_both)
    down_stays = final_product(after(cot_columns, d_attn), hidden_both)
    early = (gain_two_part, out_0, out_2)
    near, one = after(near, *early), after(one, *early)
    far = along(one, MIDDLE)
    two = exchange(near, out_3)
    d_mixed_0 = dot_nt(after(d_attn, one), w_out).astype(BF)
    d_mixed_1 = dot_nt(after(one, d_mixed_0), w_out).astype(BF)
    far, two = after(far, d_mixed_1), after(two, d_mixed_1)
    three = exchange(far, out_2)
    slot_2 = jnp.where(is_middle, near, two)
    d_mixed_2 = dot_nt(slot_2, w_out).astype(BF)
    out_across = along(out_3 + after(two, d_mixed_2), MIDDLE)
    before = attention_back(
        places, bound, qkv, jnp.concatenate([d_mixed_0, d_mixed_1, d_mixed_2], axis=0), 0, None
    )
    feed_got = [after(g, d_mixed_1) for g in feed_got]
    feed_gots = [[g] for g in feed_got]
    down_gots = [[g] for g in down_got]
    rests = []
    for stage in range(1, len(order_one)):
        rest = [
            jnp.concatenate(
                [
                    half_sums(second_columns, feed_both, side, stage, feed_gots[side]),
                    half_sums(cot_columns, hidden_both, side, stage, down_gots[side]),
                ],
                axis=1,
            ).astype(BF)
            for side in (0, 1)
        ]
        rest_got = [after(got, before[0]) for got in send_halves(rest, stage)]
        rests.append(rest_got)
        for side, got in enumerate(rest_got):
            feed_gots[side].append(got[:, : d_feed.shape[1]])
            down_gots[side].append(got[:, d_feed.shape[1] :])
    three = after(three, before[0])
    slot_3 = jnp.where(is_middle, far, three)
    d_mixed_3 = dot_nt(slot_3, w_out).astype(BF)
    d_qkv = attention_back(places, bound, qkv, d_mixed_3, 3 * shard, before)

    third = dot_nt(rows_of(d_qkv, 3), w_qkv).astype(BF)
    edge = along(third, INWARD)
    qkv_both = both_rows(after(d_qkv, third))
    second = dot_nt(after(rows_of(d_qkv, 2), third), w_qkv).astype(BF)
    first = dot_nt(after(rows_of(d_qkv, 1), third), w_qkv)
    zeroth = dot_nt(after(rows_of(d_qkv, 0), third), w_qkv)
    out_middle = along(after(out_2 + three, second), MIDDLE)
    out_sum = (out_1 + after(out_across, second).astype(F32)).astype(BF)
    d_normed_part = jnp.concatenate([zeroth, first, second.astype(F32), third.astype(F32)], axis=0)
    gain_one_part = jnp.sum(d_normed_part * normed_full.astype(F32), axis=0)
    gains = jnp.stack([gain_one_part / gain_attn, gain_two_part])
    gains = gains + swap_dp(gains, bits[0])
    gains_got = swap_dp(gains, bits[1])
    of_qkv = (normed_blocks, after(qkv_both, gains), 0, order_one)
    qkv_go = block_sums(*of_qkv, []).astype(BF)
    qkv_got = swap_dp(qkv_go, order_one[0])
    edge = after(edge, out_sum, gains, *rest_got)
    across = along(third + edge, MIDDLE)
    edge_two = exchange(out_sum, after(second, edge))
    gains = gains + after(gains_got, edge, qkv_go)
    for bit in bits[2:]:
        gains = gains + swap_dp(gains, bit)
    attn_full = jnp.concatenate([d_attn, one, slot_2, slot_3], axis=0)
    attn_blocks = column_blocks(after(attn_full, third))
    of_out = (attn_blocks, mixed_both, 1, order_two)
    out_go = block_sums(*of_out, []).astype(BF)
    out_got = swap_dp(out_go, order_two[0])
    across, edge_two = after(across, out_go), after(edge_two, out_go)
    gains_there = gains
    gains = gains.astype(BF)
    pair = along(
        jnp.concatenate([(first + across.astype(F32)).astype(BF), gains], axis=0), PAIRS
    )
    middle = along(second + edge_two, MIDDLE)
    qkv_gots = [after(qkv_got, across)]
    qkv_mid = pass_on(of_qkv, qkv_gots)
    out_gots = [after(out_got, across)]
    out_back = pass_on(of_out, out_gots)
    gains = gains.astype(F32) + pair[shard:].astype(F32)
    gains = gains + along(gains, [(i, i ^ 2) for i in range(4)])
    pair = pair[:shard]
    down_late = [
        [after(down_gots[side][0], qkv_mid)]
        + [after(r[side], qkv_mid)[:, d_feed.shape[1] :] for r in rests]
        for side in (0, 1)
    ]
    grad_down = final_rows(down_stays, down_late).T
    feed_late = [
        [after(feed_gots[side][0], qkv_go)]
        + [after(r[side], qkv_go)[:, : d_feed.shape[1]] for r in rests]
        for side in (0, 1)
    ]
    grad_feed = final_rows(feed_stays, feed_late)
    qkv_stays = dot_tn(take(after(of_qkv[0], qkv_mid), even_slots, [0], 1), of_qkv[1])
    out_stays = dot_tn(mixed_both, take(after(attn_blocks, qkv_mid), even_slots, [0], 1))
    grad_qkv = block_sums(*of_qkv, qkv_gots, qkv_stays)
    grad_out = block_sums(*of_out, out_gots, out_stays)
    out_rest = jnp.where(
        is_middle, out_in.astype(F32) + after(out_middle, across).astype(F32), edge_two.astype(F32)
    )
    outputs = (resid + (out_0 + out_rest)).astype(BF)
    d_normed = zeroth + pair.astype(F32) + middle.astype(F32)
    weighted_one = d_normed * gain_attn
    grad_tokens = (
        d_resid
        + scale_one * weighted_one
        - inputs * scale_one**3 * jnp.mean(weighted_one * inputs, axis=-1, keepdims=True)
    )
    return (
        outputs,
        grad_tokens,
        grad_qkv[:, :n_q],
        grad_qkv[:, n_q : 2 * n_q],
        grad_qkv[:, 2 * n_q :],
        grad_out,
        grad_feed[:, :units],
        grad_feed[:, wide : wide + units],
        grad_down,
        gains[0],
        gains[1],
    )


def solution(mesh):
    return jax.shard_map(
        on_device,
        mesh=mesh,
        in_specs=(
            P(("dp", "mp"), None),
            P("dp"),
            P(None, "mp"),
            P(None, "mp"),
            P(None, "mp"),
            P("mp", None),
            P(None, "mp"),
            P(None, "mp"),
            P("mp", None),
            P(),
            P(),
            P(("dp", "mp"), None),
        ),
        out_specs=(
            P(("dp", "mp"), None),
            P(("dp", "mp"), None),
            P("dp", "mp"),
            P("dp", "mp"),
            P("dp", "mp"),
            P("mp", "dp"),
            P("dp", "mp"),
            P("dp", "mp"),
            P("mp", "dp"),
            P(),
            P(),
        ),
        check_vma=False,
    )
```
